512 devices in a mesh: tm: 2 (over core), space: 256 (over z, y, x).
Axes of the slice: x: 4, y: 8, z: 8, core: 2. Of those that a mesh axis runs over, the one named last changes fastest.
Arguments:
- adj_source: float32 [32, 2, 131072], P('tm', None, 'space'), may hold values from -4 to 6
- terminal: float32 [2, 131072], P(None, 'space'), may hold values from -4 to 6
- capacity: float32 [131072], P('space'), may hold values from 0.2 to 2
- blocks: float32 [2048, 7, 64, 64], P('space'), as said below
- columns: int32 [2048, 7], P('space'), may hold values from 0 to 15, as said below
- face_lists: int32 [256, 2, 4], P('space'), may hold values from 0 to 7, as said below
Outputs:
- adjoint: float32 [32, 2, 131072], P('tm', None, 'space')
The draws below stay inside these ranges and needn't reach their ends.
Inputs may be any that keep to these rules, and one draw needn't show every extreme that they name: `columns`: entry 0 of each block row is the row's own block (local id R mod 8); entry 1 is one of the 8 received blocks; ids may repeat within a row. `face_lists`: each list holds 4 distinct own blocks; the two lists of a shard are disjoint; block 0 is always sent to the lower shard and block 7 to the upper one. `blocks`: in every row of a block row, the diagonal entry of the own block exceeds the sum of magnitudes of all other entries of that row.
All inputs are finite; a program needn't handle non-finite values.
Results may differ from the reference program's by a relative error of at most 0.0001.
Values sent between devices are 32-bit elements; how exact they have to be, the bound alone decides.
A program may use at most 64 MiB of HBM per device.

```python
import math
import jax
import jax.numpy as jnp
from jax import lax

BLOCK = 64
NNZ = 7
STEPS = 32
CASES = 2
OUTER = 3
SWEEPS = 3
HALO = 4
NB_DEV = 8
SHARDS = 256
NBLK = 2048
NODES = 131072


def draw_blocks(key, part):
    own_key = jax.random.fold_in(key, 5)
    key_couple, key_margin, key_contact, key_link = jax.random.split(own_key, 4)
    amplitude = 0.8
    margin_low = 0.05
    margin_high = 0.25
    rough = jax.random.uniform(key_couple, (NBLK, NNZ, BLOCK, BLOCK), jnp.float32, 0.0, 1.0)
    beside = jnp.roll(rough, 1, axis=3)
    weak = -(1.0 + amplitude * (rough - beside)) * (0.1 / ((NNZ - 1) * BLOCK))
    pick = jax.random.randint(key_contact, (NBLK, BLOCK, BLOCK // 8), 0, 8, dtype=jnp.int32)
    onehot = (pick[..., None] == jnp.arange(8, dtype=jnp.int32)).reshape(NBLK, BLOCK, BLOCK).astype(jnp.float32)
    link_rough = jax.random.uniform(key_link, (NBLK, BLOCK, BLOCK), jnp.float32, 0.0, 1.0)
    link_spread = link_rough - jnp.roll(link_rough, 1, axis=2)
    strong = -(0.2 + 6.4 * onehot + 0.2 * link_spread) * (0.9 / BLOCK)
    entry_ids = jnp.arange(NNZ, dtype=jnp.int32)[None, :, None, None]
    coupling = jnp.where(entry_ids == 1, strong[:, None], weak)
    margin = jnp.exp(jax.random.uniform(key_margin, (NBLK, 1, BLOCK, 1), jnp.float32, math.log(margin_low), math.log(margin_high)))
    diagonal = 1.0 + margin
    self_mask = (entry_ids == 0) & jnp.eye(BLOCK, dtype=bool)[None, None]
    return jnp.where(self_mask, diagonal, coupling).astype(jnp.float32)


def smooth_part(key, step_count, level_low, level_high):
    key_level, key_space, key_time = jax.random.split(key, 3)
    level = jax.random.uniform(key_level, (1, CASES, 1), jnp.float32, level_low, level_high)
    space_phase = jax.random.uniform(key_space, (1, CASES, 1), jnp.float32, 0.0, 2.0 * math.pi)
    time_phase = jax.random.uniform(key_time, (1, CASES, 1), jnp.float32, 0.0, 2.0 * math.pi)
    node_pos = (jnp.arange(NODES, dtype=jnp.int32).astype(jnp.float32) / NODES)[None, None, :]
    step_pos = (jnp.arange(step_count, dtype=jnp.int32).astype(jnp.float32) / STEPS)[:, None, None]
    space_wave = 1.0 + 0.5 * jnp.sin(2.0 * math.pi * 3.0 * node_pos + space_phase)
    time_wave = 1.0 + 0.3 * jnp.cos(2.0 * math.pi * step_pos + time_phase)
    return level * space_wave * time_wave


def draw_adj_source(key, part):
    own_key = jax.random.fold_in(key, 11)
    key_noise, key_smooth = jax.random.split(own_key)
    noise = jnp.clip(jax.random.normal(key_noise, (STEPS, CASES, NODES), jnp.float32), -4.0, 4.0)
    smooth = smooth_part(key_smooth, STEPS, 0.3, 0.6)
    return (noise + smooth).astype(jnp.float32)


def draw_terminal(key, part):
    own_key = jax.random.fold_in(key, 23)
    key_noise, key_smooth = jax.random.split(own_key)
    noise = jnp.clip(jax.random.normal(key_noise, (CASES, NODES), jnp.float32), -4.0, 4.0)
    smooth = smooth_part(key_smooth, 1, 0.3, 0.6)[0]
    return (noise + smooth).astype(jnp.float32)


def draw_columns(key, part):
    rows = jnp.arange(NBLK, dtype=jnp.int32) % NB_DEV
    face_col = NB_DEV + rows % (2 * HALO)
    others = jax.random.randint(key, (NBLK, NNZ - 2), 0, NB_DEV + 2 * HALO, dtype=jnp.int32)
    return jnp.concatenate([rows[:, None], face_col[:, None], others], axis=1).astype(jnp.int32)


def draw_face_lists(key, part):
    own_key = jax.random.fold_in(key, 31)
    shard_keys = jax.random.split(own_key, SHARDS)

    def per_shard(shard_key):
        shuffled = jax.random.permutation(shard_key, NB_DEV - 2).astype(jnp.int32) + 1
        lower_list = jnp.concatenate([jnp.zeros((1,), jnp.int32), shuffled[:HALO - 1]])
        upper_list = jnp.concatenate([jnp.full((1,), NB_DEV - 1, jnp.int32), shuffled[HALO - 1:2 * HALO - 2]])
        return jnp.stack([lower_list, upper_list])
    return jax.vmap(per_shard)(shard_keys).astype(jnp.int32)


def levels(key, extent, cuts, least, high):
    def one(axis_at, blocks):
        heights = jax.random.uniform(jax.random.fold_in(jax.random.fold_in(key, 6), axis_at), (blocks,), jnp.float32, least / len(cuts), high / len(cuts))
        return jnp.repeat(jnp.exp(heights), extent[axis_at] // blocks).reshape((-1,) + (1,) * (len(extent) - axis_at - 1))

    factor_of = one(*cuts[0])
    for cut in cuts[1:]:
        factor_of = factor_of * one(*cut)
    return factor_of


def setup_inputs(seed: int = 0) -> dict:
    streams_of = jax.random.split(jax.random.key(seed), 7)
    adj_source = draw_adj_source(jax.random.fold_in(streams_of[6], 71), 0)
    terminal = draw_terminal(jax.random.fold_in(streams_of[6], 71), 0)
    capacity = jnp.clip(jnp.exp(math.log(2.0) - 2.3025851 * jax.random.uniform(streams_of[2], (NODES,), jnp.float32) ** levels(streams_of[2], (NODES,), ((0, 256),), -0.2, 0.2)), 0.2, 2.0)
    blocks = draw_blocks(jax.random.fold_in(streams_of[6], 71), 0)
    columns = draw_columns(jax.random.fold_in(streams_of[6], 71), 0)
    face_lists = draw_face_lists(jax.random.fold_in(streams_of[6], 71), 0)
    return {"adj_source": adj_source, "terminal": terminal, "capacity": capacity, "blocks": blocks, "columns": columns, "face_lists": face_lists}


CORNER_WEIGHT = 0.1
EXACT_PRECISION = lax.Precision.HIGHEST


def forward_matrix(mode_start, mode_count, step_start, step_count, step_total):
    mode_ids = mode_start + jnp.arange(mode_count, dtype=jnp.int32)
    time_ids = step_start + jnp.arange(step_count, dtype=jnp.int32)
    angles = ((mode_ids[:, None] * time_ids[None, :]) % step_total).astype(jnp.float32) * (2.0 * math.pi / step_total)
    return jnp.stack([jnp.cos(angles), -jnp.sin(angles)], axis=1)


def inverse_matrix(mode_start, mode_count, step_start, step_count, step_total):
    mode_ids = mode_start + jnp.arange(mode_count, dtype=jnp.int32)
    time_ids = step_start + jnp.arange(step_count, dtype=jnp.int32)
    angles = ((time_ids[:, None] * mode_ids[None, :]) % step_total).astype(jnp.float32) * (2.0 * math.pi / step_total)
    return jnp.stack([jnp.cos(angles), -jnp.sin(angles)], axis=2) / step_total


def complex_product(left_real, left_imag, right_real, right_imag):
    return left_real * right_real - left_imag * right_imag, left_real * right_imag + left_imag * right_real


def apply_conduct(field, blocks, columns, face_lists):
    column_count = field.shape[0]
    shaped = jnp.moveaxis(field.reshape(column_count, SHARDS, NB_DEV, BLOCK), 1, 0)
    take_rows = jax.vmap(lambda shard_field, block_ids: jnp.take(shard_field, block_ids, axis=1))
    to_lower = take_rows(shaped, face_lists[:, 0])
    to_upper = take_rows(shaped, face_lists[:, 1])
    zero_rows = jnp.zeros_like(to_lower[:1])
    from_lower = jnp.concatenate([zero_rows, to_upper[:-1]], axis=0)
    from_upper = jnp.concatenate([to_lower[1:], zero_rows], axis=0)
    extended = jnp.concatenate([shaped, from_lower, from_upper], axis=2)
    shard_blocks = blocks.reshape(SHARDS, NB_DEV, NNZ, BLOCK, BLOCK)
    shard_cols = columns.reshape(SHARDS, NB_DEV, NNZ)

    def per_shard(entry):
        shard_ext, shard_blk, shard_col = entry
        gathered = jnp.take(shard_ext, shard_col, axis=1)
        return jnp.einsum("crkp,rkqp->crq", gathered, shard_blk, precision=EXACT_PRECISION)

    result = lax.map(per_shard, (extended, shard_blocks, shard_cols))
    return jnp.moveaxis(result, 0, 1).reshape(column_count, SHARDS * NB_DEV * BLOCK)


def reference(adj_source, terminal, capacity, blocks, columns, face_lists):
    times = jnp.arange(STEPS, dtype=jnp.int32).astype(jnp.float32)
    forward_scale = jnp.power(CORNER_WEIGHT, times / STEPS)
    backward_scale = jnp.power(CORNER_WEIGHT, -times / STEPS)
    root_weight = CORNER_WEIGHT ** (1.0 / STEPS)
    mode_angles = times * (2.0 * math.pi / STEPS)
    real_coef = 1.0 - root_weight * jnp.cos(mode_angles)
    imag_coef = root_weight * jnp.sin(mode_angles)
    own_diagonal = jnp.diagonal(blocks[:, 0], axis1=1, axis2=2).reshape(NODES)
    denom_real = real_coef[:, None] * capacity[None, :] + own_diagonal[None, :]
    denom_imag = imag_coef[:, None] * capacity[None, :]
    magnitude = denom_real * denom_real + denom_imag * denom_imag
    recip_real = (denom_real / magnitude)[:, None, :]
    recip_imag = (-denom_imag / magnitude)[:, None, :]
    coef_real = real_coef[:, None, None]
    coef_imag = imag_coef[:, None, None]
    forward_table = forward_matrix(0, STEPS, 0, STEPS, STEPS).reshape(2 * STEPS, STEPS)
    inverse_table = inverse_matrix(0, STEPS, 0, STEPS, STEPS).reshape(STEPS, 2 * STEPS)
    solution = jnp.zeros((STEPS, CASES, NODES), jnp.float32)
    for outer_step in range(OUTER):
        previous = jnp.concatenate([terminal[None], solution[:-1]], axis=0)
        conducted = apply_conduct(solution.reshape(STEPS * CASES, NODES), blocks, columns, face_lists).reshape(STEPS, CASES, NODES)
        resid = adj_source - capacity * (solution - previous) - conducted
        scaled = resid * forward_scale[:, None, None]
        spectrum = jnp.dot(forward_table, scaled.reshape(STEPS, -1), precision=EXACT_PRECISION).reshape(STEPS, 2, CASES, NODES)
        spec_real = spectrum[:, 0]
        spec_imag = spectrum[:, 1]
        value_real, value_imag = complex_product(recip_real, recip_imag, spec_real, spec_imag)
        for sweep in range(SWEEPS - 1):
            stacked = jnp.stack([value_real, value_imag], axis=1)
            conducted_modes = apply_conduct(stacked.reshape(STEPS * 2 * CASES, NODES), blocks, columns, face_lists).reshape(STEPS, 2, CASES, NODES)
            held_real = capacity * (coef_real * value_real - coef_imag * value_imag)
            held_imag = capacity * (coef_imag * value_real + coef_real * value_imag)
            resid_real = spec_real - held_real - conducted_modes[:, 0]
            resid_imag = spec_imag - held_imag - conducted_modes[:, 1]
            step_real, step_imag = complex_product(recip_real, recip_imag, resid_real, resid_imag)
            value_real = value_real + step_real
            value_imag = value_imag + step_imag
        modes = jnp.stack([value_real, value_imag], axis=1)
        update = jnp.dot(inverse_table, modes.reshape(2 * STEPS, -1), precision=EXACT_PRECISION).reshape(STEPS, CASES, NODES)
        solution = solution + update * backward_scale[:, None, None]
    return solution
```

```python
import functools
import math

import jax
import jax.numpy as jnp
import numpy as np
from jax import lax
from jax.experimental import pallas as pl
from jax.experimental.pallas import tpu as pltpu
from jax.sharding import PartitionSpec as P

OUTER = 3
SWEEPS = 3
STEPS = 32
HALF = STEPS // 2
CORNER_WEIGHT = 0.1
ROOT = CORNER_WEIGHT ** (1.0 / STEPS)
ROUNDS = OUTER * SWEEPS - 1
BLOCK = 64
LANES = 128
MESH = pl.DeviceIdType.MESH


def split(value):
    high = value.astype(jnp.bfloat16)
    low = (value - high.astype(jnp.float32)).astype(jnp.bfloat16)
    return high, low


def split_table(table):
    high = table.astype(jnp.bfloat16)
    low = (table - high.astype(np.float64)).astype(jnp.bfloat16)
    return np.concatenate([high, high, low], axis=1)


def tables():
    steps = np.arange(STEPS)
    modes = np.arange(HALF)
    angles = 2.0 * np.pi * ((modes[:, None] * steps[None, :]) % STEPS) / STEPS
    nyquist = (-1.0) ** steps
    cosines, sines = np.cos(angles), -np.sin(angles)
    sines[0] = nyquist
    basis = np.concatenate([cosines, sines], axis=0)
    scale = CORNER_WEIGHT ** (steps / STEPS)
    forward = basis * scale[None, :]
    weight = np.full((STEPS,), 2.0)
    weight[0] = weight[HALF] = 1.0
    inverse = (basis * weight[:, None]).T / STEPS
    last = inverse[STEPS - 1] * ROOT
    backward = inverse / scale[:, None]
    real_coef = 1.0 - ROOT * np.cos(2.0 * np.pi * modes / STEPS)
    imag_coef = ROOT * np.sin(2.0 * np.pi * modes / STEPS)
    real_low = real_coef.copy()
    real_low[0] = 1.0 + ROOT
    columns = np.zeros((STEPS, LANES), np.float32)
    columns[:HALF, 0] = real_coef
    columns[HALF:, 0] = real_low
    columns[:HALF, 1] = imag_coef
    columns[:, 2] = last
    return split_table(forward), split_table(backward), columns


def product(table, value):
    high, low = split(value)
    return jnp.dot(
        table, jnp.concatenate([high, low, high], axis=0), preferred_element_type=jnp.float32
    )


def reorder(value, ids):
    lower_half = lax.broadcasted_iota(jnp.int32, (1, LANES), 1) < BLOCK
    both = []
    for tile in range(4):
        plain = value[:, tile * LANES : (tile + 1) * LANES]
        turned = pltpu.roll(plain, BLOCK, 1)
        both.append(jnp.where(lower_half, plain, turned))
        both.append(jnp.where(lower_half, turned, plain))
    tiles = []
    for tile in range(4):
        wanted = jnp.where(lower_half, ids[2 * tile], ids[2 * tile + 1])
        total = both[0]
        for block in range(1, 8):
            total = jnp.where(wanted == block, both[block], total)
        tiles.append(total)
    return jnp.concatenate(tiles, axis=1)


def kernel(
    adj, term, cap, cols, faces, forward, backward, coefs, blocks_hbm, out,
    blk, turned, mat_high, mat_low, diag, recip, capacity, xsend, xrecv, wsend, wrecv,
    total, ysend, yrecv, blk_sem, tm_sems, send_sems, recv_sems,
):
    group = lax.axis_index("tm")
    shard = lax.axis_index("space")
    shards = lax.axis_size("space")
    other = 1 - group
    lower = lax.rem(shard + shards - 1, shards)
    upper = lax.rem(shard + 1, shards)
    first = group == 0

    blk_copy = pltpu.make_async_copy(blocks_hbm, blk, blk_sem)
    blk_copy.start()

    barrier = pltpu.get_barrier_semaphore()
    for target in ((other, shard), (group, lower), (group, upper)):
        pl.semaphore_signal(barrier, inc=1, device_id=target, device_id_type=MESH)
    case_0 = adj[:, 0, :]
    case_1 = adj[:, 1, :]
    xsend[...] = jnp.where(first, case_1, case_0)
    mine = jnp.where(first, case_0, case_1)
    pl.semaphore_wait(barrier, 3)

    xcopy = pltpu.make_async_remote_copy(
        src_ref=xsend, dst_ref=xrecv, send_sem=tm_sems.at[0], recv_sem=tm_sems.at[1],
        device_id=(other, shard), device_id_type=MESH,
    )
    xcopy.start()

    ids = [faces[i // 4, i % 4] for i in range(8)]
    cap_row = cap[...]
    capacity[...] = reorder(jnp.broadcast_to(cap_row, (8, 8 * BLOCK)), ids)
    blk_copy.wait()
    eye = lax.broadcasted_iota(jnp.int32, (BLOCK, BLOCK), 0) == lax.broadcasted_iota(
        jnp.int32, (BLOCK, BLOCK), 1
    )
    rows = [
        jnp.sum(jnp.where(eye, blk[ids[i], 0], 0.0), axis=0, keepdims=True) for i in range(8)
    ]
    diag[...] = jnp.broadcast_to(jnp.concatenate(rows, axis=1), diag.shape)
    cap_own = capacity[0:1, :]
    diag_own = diag[0:1, :]
    imag = coefs[0:HALF, 1:2] * cap_own
    for part in range(2):
        real = coefs[part * HALF : (part + 1) * HALF, 0:1] * cap_own + diag_own
        over = 1.0 / (real * real + imag * imag)
        recip[part] = real * over
        if part == 0:
            recip[2] = -imag * over

    def divided(value):
        upper_part, lower_part = value[:HALF], value[HALF:]
        return jnp.concatenate(
            [
                recip[0] * upper_part - recip[2] * lower_part,
                recip[2] * upper_part + recip[1] * lower_part,
            ],
            axis=0,
        )

    def halo(slot):
        down = pltpu.make_async_remote_copy(
            src_ref=wsend.at[slot, 0], dst_ref=wrecv.at[slot, 1],
            send_sem=send_sems.at[slot, 0], recv_sem=recv_sems.at[slot, 1],
            device_id=(group, lower), device_id_type=MESH,
        )
        up = pltpu.make_async_remote_copy(
            src_ref=wsend.at[slot, 1], dst_ref=wrecv.at[slot, 0],
            send_sem=send_sems.at[slot, 1], recv_sem=recv_sems.at[slot, 0],
            device_id=(group, upper), device_id_type=MESH,
        )
        return down, up

    def send(slot, value):
        wsend[slot, 0] = value[:, : 4 * BLOCK]
        wsend[slot, 1] = value[:, 4 * BLOCK :]
        down, up = halo(slot)
        down.start()
        up.start()

    xcopy.wait()
    theirs = xrecv[...]
    source = jnp.concatenate(
        [jnp.where(first, mine, theirs), jnp.where(first, theirs, mine)], axis=0
    )
    head = jnp.where(first, term[0:1, :], term[1:2, :]) * cap_row
    row_ids = lax.broadcasted_iota(jnp.int32, (STEPS, 1), 0)
    source = source + jnp.where(row_ids == 0, head, 0.0)
    spectrum = reorder(product(forward[...], source), ids)
    field = divided(spectrum)
    send(0, field)
    total[...] = jnp.zeros_like(total)

    lower_half = lax.broadcasted_iota(jnp.int32, (1, LANES), 1) < BLOCK
    turned_eye = lax.broadcasted_iota(jnp.int32, (BLOCK, LANES), 0) == lax.rem(
        lax.broadcasted_iota(jnp.int32, (BLOCK, LANES), 1), BLOCK
    )
    no_lower = shard == 0
    no_upper = shard == shards - 1
    for pair in range(4):
        left, right = ids[2 * pair], ids[2 * pair + 1]
        wanted = []
        for k in range(7):
            entry = jnp.concatenate([blk[left, k], blk[right, k]], axis=0)
            entry = -entry.T
            if k == 0:
                entry = jnp.where(turned_eye, 0.0, entry)
            turned[k] = entry
            wanted.append(jnp.where(lower_half, cols[left, k], cols[right, k]))
        for place in range(16):
            if place < 8:
                name = ids[place]
            elif place < 12:
                name = jnp.where(no_lower, -1, place)
            else:
                name = jnp.where(no_upper, -1, place)
            tile = jnp.where(wanted[0] == name, turned[0], 0.0)
            for k in range(1, 7):
                tile = tile + jnp.where(wanted[k] == name, turned[k], 0.0)
            high, low = split(tile)
            where = (slice(place * BLOCK, (place + 1) * BLOCK), slice(pair * LANES, (pair + 1) * LANES))
            mat_high[where] = high
            mat_low[where] = low

    def conduct(value, start, count):
        high, low = split(value)
        both = jnp.dot(
            jnp.concatenate([high, low], axis=0), mat_high[start : start + count, :],
            preferred_element_type=jnp.float32,
        )
        rest = jnp.dot(
            high, mat_low[start : start + count, :], preferred_element_type=jnp.float32
        )
        return both[:STEPS] + both[STEPS:] + rest

    real_rows = row_ids <= HALF
    last = coefs[:, 2:3]

    def round_of(slot, tail):
        value = jnp.concatenate([wsend[slot, 0], wsend[slot, 1]], axis=1)
        total[...] += value
        tail = tail + jnp.sum(value * last, axis=0, keepdims=True)
        closes = lax.rem(slot, SWEEPS) == SWEEPS - 1
        fix = jnp.where(closes, tail, 0.0) * capacity[0:1, :]
        tail = jnp.where(closes, 0.0, tail)
        result = conduct(value, 0, 8 * BLOCK) - jnp.where(real_rows, fix, 0.0)
        down, up = halo(slot)
        up.wait_recv()
        result = result + conduct(wrecv[slot, 0], 8 * BLOCK, 4 * BLOCK)
        down.wait_recv()
        result = result + conduct(wrecv[slot, 1], 12 * BLOCK, 4 * BLOCK)
        down.wait_send()
        up.wait_send()
        return divided(result), tail

    def step(slot, tail):
        value, tail = round_of(slot, tail)
        send(slot + 1, value)
        return tail

    tail = lax.fori_loop(0, ROUNDS - 1, step, jnp.zeros((1, 8 * BLOCK), jnp.float32))
    value, _ = round_of(ROUNDS - 1, tail)

    places = []
    for block in range(8):
        place = jnp.int32(0)
        for i in range(1, 8):
            place = place + jnp.where(ids[i] == block, i, 0)
        places.append(place)
    summed = product(backward[...], reorder(total[...] + value, places))
    early, late = summed[:HALF], summed[HALF:]
    ysend[...] = jnp.where(first, late, early)
    ycopy = pltpu.make_async_remote_copy(
        src_ref=ysend, dst_ref=yrecv, send_sem=tm_sems.at[2], recv_sem=tm_sems.at[3],
        device_id=(other, shard), device_id_type=MESH,
    )
    ycopy.start()
    kept = jnp.where(first, early, late)
    ycopy.wait()
    came = yrecv[...]
    out[:, 0, :] = jnp.where(first, kept, came)
    out[:, 1, :] = jnp.where(first, came, kept)


def per_device(adj_source, terminal, capacity, blocks, columns, face_lists):
    nodes = capacity.shape[0]
    forward, backward, coefs = tables()
    vmem = pl.BlockSpec(memory_space=pltpu.VMEM)
    smem = pl.BlockSpec(memory_space=pltpu.SMEM)
    f32, bf16 = jnp.float32, jnp.bfloat16
    return pl.pallas_call(
        kernel,
        out_shape=jax.ShapeDtypeStruct(adj_source.shape, f32),
        in_specs=[vmem, vmem, vmem, smem, smem, vmem, vmem, vmem, pl.BlockSpec(memory_space=pl.ANY)],
        out_specs=vmem,
        scratch_shapes=[
            pltpu.VMEM(blocks.shape, f32),
            pltpu.VMEM((7, BLOCK, LANES), f32),
            pltpu.VMEM((16 * BLOCK, nodes), bf16),
            pltpu.VMEM((16 * BLOCK, nodes), bf16),
            pltpu.VMEM((8, nodes), f32),
            pltpu.VMEM((3, HALF, nodes), f32),
            pltpu.VMEM((8, nodes), f32),
            pltpu.VMEM((HALF, nodes), f32),
            pltpu.VMEM((HALF, nodes), f32),
            pltpu.VMEM((ROUNDS, 2, STEPS, nodes // 2), f32),
            pltpu.VMEM((ROUNDS, 2, STEPS, nodes // 2), f32),
            pltpu.VMEM((STEPS, nodes), f32),
            pltpu.VMEM((HALF, nodes), f32),
            pltpu.VMEM((HALF, nodes), f32),
            pltpu.SemaphoreType.DMA,
            pltpu.SemaphoreType.DMA((4,)),
            pltpu.SemaphoreType.DMA((ROUNDS, 2)),
            pltpu.SemaphoreType.DMA((ROUNDS, 2)),
        ],
        compiler_params=pltpu.CompilerParams(
            collective_id=0, has_side_effects=True, vmem_limit_bytes=24 * 1024 * 1024
        ),
        name="window",
    )(
        adj_source, terminal, capacity.reshape(1, nodes), columns, face_lists.reshape(2, 4),
        jnp.asarray(forward), jnp.asarray(backward), jnp.asarray(coefs), blocks,
    )


def solution(mesh):
    return jax.shard_map(
        per_device,
        mesh=mesh,
        in_specs=(
            P("tm", None, "space"),
            P(None, "space"),
            P("space"),
            P("space", None, None, None),
            P("space", None),
            P("space", None, None),
        ),
        out_specs=P("tm", None, "space"),
        check_vma=False,
    )
```

```python
import functools
import math

import jax
import jax.numpy as jnp
import numpy as np
from jax import lax
from jax.experimental import pallas as pl
from jax.experimental.pallas import tpu as pltpu
from jax.sharding import PartitionSpec as P

OUTER = 3
SWEEPS = 3
STEPS = 32
HALF = STEPS // 2
CORNER_WEIGHT = 0.1
ROOT = CORNER_WEIGHT ** (1.0 / STEPS)
ROUNDS = OUTER * SWEEPS - 1
BLOCK = 64
LANES = 128
MESH = pl.DeviceIdType.MESH


def split(value):
    high = value.astype(jnp.bfloat16)
    low = (value - high.astype(jnp.float32)).astype(jnp.bfloat16)
    return high, low


def split_table(table):
    high = table.astype(jnp.bfloat16)
    low = (table - high.astype(np.float64)).astype(jnp.bfloat16)
    return np.concatenate([high, high, low], axis=1)


def tables():
    steps = np.arange(STEPS)
    modes = np.arange(HALF)
    angles = 2.0 * np.pi * ((modes[:, None] * steps[None, :]) % STEPS) / STEPS
    nyquist = (-1.0) ** steps
    cosines, sines = np.cos(angles), -np.sin(angles)
    sines[0] = nyquist
    basis = np.concatenate([cosines, sines], axis=0)
    scale = CORNER_WEIGHT ** (steps / STEPS)
    forward = basis * scale[None, :]
    weight = np.full((STEPS,), 2.0)
    weight[0] = weight[HALF] = 1.0
    inverse = (basis * weight[:, None]).T / STEPS
    last = inverse[STEPS - 1] * ROOT
    backward = inverse / scale[:, None]
    real_coef = 1.0 - ROOT * np.cos(2.0 * np.pi * modes / STEPS)
    imag_coef = ROOT * np.sin(2.0 * np.pi * modes / STEPS)
    real_low = real_coef.copy()
    real_low[0] = 1.0 + ROOT
    columns = np.zeros((STEPS, LANES), np.float32)
    columns[:HALF, 0] = real_coef
    columns[HALF:, 0] = real_low
    columns[:HALF, 1] = imag_coef
    columns[:, 2] = last
    halves = [split_table(forward[:, part * HALF : (part + 1) * HALF]) for part in range(2)]
    return np.stack(halves), split_table(backward), columns


def product(table, value):
    high, low = split(value)
    return jnp.dot(
        table, jnp.concatenate([high, low, high], axis=0), preferred_element_type=jnp.float32
    )


def reorder(value, ids):
    lower_half = lax.broadcasted_iota(jnp.int32, (1, LANES), 1) < BLOCK
    both = []
    for tile in range(4):
        plain = value[:, tile * LANES : (tile + 1) * LANES]
        turned = pltpu.roll(plain, BLOCK, 1)
        both.append(jnp.where(lower_half, plain, turned))
        both.append(jnp.where(lower_half, turned, plain))
    tiles = []
    for tile in range(4):
        wanted = jnp.where(lower_half, ids[2 * tile], ids[2 * tile + 1])
        total = both[0]
        for block in range(1, 8):
            total = jnp.where(wanted == block, both[block], total)
        tiles.append(total)
    return jnp.concatenate(tiles, axis=1)


def kernel(
    adj_hbm, term_hbm, cap_hbm, cols_hbm, faces_hbm, forward_hbm, backward_hbm, coefs_hbm,
    blocks_hbm, out,
    adj, term, cap, cols, faces, forward, backward, coefs, blk,
    turned, mat_high, mat_low, diag, recip, capacity, psend, precv, pown, wsend, wrecv,
    total, ysend, yrecv, load_sems, first_send, first_recv, last_sems, send_sems, recv_sems,
):
    group = lax.axis_index("tm")
    shard = lax.axis_index("space")
    shards = lax.axis_size("space")
    other = 1 - group
    has_lower = shard > 0
    has_upper = shard < shards - 1
    lower = jnp.maximum(shard - 1, 0)
    upper = jnp.minimum(shard + 1, shards - 1)
    first = group == 0

    barrier = pltpu.get_barrier_semaphore()

    def greet(target):
        pl.semaphore_signal(barrier, inc=1, device_id=target, device_id_type=MESH)

    @pl.when(has_lower)
    def _():
        greet((0, lower))
        greet((1, lower))

    @pl.when(has_upper)
    def _():
        greet((0, upper))
        greet((1, upper))

    greet((other, shard))

    loads = [
        pltpu.make_async_copy(source, target, load_sems.at[i])
        for i, (source, target) in enumerate(
            [
                (faces_hbm, faces), (cols_hbm, cols), (adj_hbm, adj), (term_hbm, term),
                (cap_hbm, cap), (coefs_hbm, coefs), (forward_hbm, forward),
                (blocks_hbm, blk), (backward_hbm, backward),
            ]
        )
    ]
    for load in loads:
        load.start()

    @pl.when(jnp.logical_not(has_lower))
    def _():
        wrecv[:, 0] = jnp.zeros_like(wrecv[:, 0])
        precv[:, 0] = jnp.zeros_like(precv[:, 0])

    @pl.when(jnp.logical_not(has_upper))
    def _():
        wrecv[:, 1] = jnp.zeros_like(wrecv[:, 1])
        precv[:, 1] = jnp.zeros_like(precv[:, 1])

    for load in loads:
        load.wait()

    ids = [faces[0, i // 4, i % 4] for i in range(8)]
    cap_row = cap[...]
    capacity[...] = reorder(jnp.broadcast_to(cap_row, (8, 8 * BLOCK)), ids)
    eye = lax.broadcasted_iota(jnp.int32, (BLOCK, BLOCK), 0) == lax.broadcasted_iota(
        jnp.int32, (BLOCK, BLOCK), 1
    )
    rows = [
        jnp.sum(jnp.where(eye, blk[ids[i], 0], 0.0), axis=0, keepdims=True) for i in range(8)
    ]
    diag[...] = jnp.broadcast_to(jnp.concatenate(rows, axis=1), diag.shape)
    cap_own = capacity[0:1, :]
    diag_own = diag[0:1, :]
    imag = coefs[0:HALF, 1:2] * cap_own
    for part in range(2):
        real = coefs[part * HALF : (part + 1) * HALF, 0:1] * cap_own + diag_own
        over = 1.0 / (real * real + imag * imag)
        recip[part] = real * over
        if part == 0:
            recip[2] = -imag * over

    def divided(value):
        upper_part, lower_part = value[:HALF], value[HALF:]
        return jnp.concatenate(
            [
                recip[0] * upper_part - recip[2] * lower_part,
                recip[2] * upper_part + recip[1] * lower_part,
            ],
            axis=0,
        )

    head_row = first & (lax.broadcasted_iota(jnp.int32, (HALF, 1), 0) == 0)
    for case in range(2):
        source = adj[:, case, :] + jnp.where(head_row, term[case : case + 1, :] * cap_row, 0.0)
        part = divided(reorder(product(forward[group], source), ids))
        psend[case, 0] = part[:, : 4 * BLOCK]
        psend[case, 1] = part[:, 4 * BLOCK :]

    def first_halo(side, case, sender):
        return pltpu.make_async_remote_copy(
            src_ref=psend.at[case, side], dst_ref=precv.at[sender, 1 - side],
            send_sem=first_send.at[2 * side + case], recv_sem=first_recv.at[2 * (1 - side) + sender],
            device_id=(case, upper if side else lower), device_id_type=MESH,
        )

    first_own = pltpu.make_async_remote_copy(
        src_ref=psend.at[other], dst_ref=pown,
        send_sem=first_send.at[4], recv_sem=first_recv.at[4],
        device_id=(other, shard), device_id_type=MESH,
    )

    lower_half = lax.broadcasted_iota(jnp.int32, (1, LANES), 1) < BLOCK
    turned_eye = lax.broadcasted_iota(jnp.int32, (BLOCK, LANES), 0) == lax.rem(
        lax.broadcasted_iota(jnp.int32, (BLOCK, LANES), 1), BLOCK
    )
    for pair in range(4):
        left, right = ids[2 * pair], ids[2 * pair + 1]
        wanted = []
        for k in range(7):
            entry = jnp.concatenate([blk[left, k], blk[right, k]], axis=0)
            entry = -entry.T
            if k == 0:
                entry = jnp.where(turned_eye, 0.0, entry)
            turned[k] = entry
            wanted.append(jnp.where(lower_half, cols[left, k], cols[right, k]))
        for place in range(16):
            if place < 8:
                name = ids[place]
            elif place < 12:
                name = jnp.where(has_lower, place, -1)
            else:
                name = jnp.where(has_upper, place, -1)
            tile = jnp.where(wanted[0] == name, turned[0], 0.0)
            for k in range(1, 7):
                tile = tile + jnp.where(wanted[k] == name, turned[k], 0.0)
            high, low = split(tile)
            where = (slice(place * BLOCK, (place + 1) * BLOCK), slice(pair * LANES, (pair + 1) * LANES))
            mat_high[where] = high
            mat_low[where] = low

    neighbours = has_lower.astype(jnp.int32) + has_upper.astype(jnp.int32)
    pl.semaphore_wait(barrier, 1 + 2 * neighbours)

    @pl.when(has_lower)
    def _():
        for case in range(2):
            first_halo(0, case, group).start()

    @pl.when(has_upper)
    def _():
        for case in range(2):
            first_halo(1, case, group).start()

    first_own.start()

    def halo(slot, side):
        return pltpu.make_async_remote_copy(
            src_ref=wsend.at[slot, side], dst_ref=wrecv.at[slot, 1 - side],
            send_sem=send_sems.at[slot, side], recv_sem=recv_sems.at[slot, 1 - side],
            device_id=(group, upper if side else lower), device_id_type=MESH,
        )

    def send(slot, value):
        wsend[slot, 0] = value[:, : 4 * BLOCK]
        wsend[slot, 1] = value[:, 4 * BLOCK :]

        @pl.when(has_lower)
        def _():
            halo(slot, 0).start()

        @pl.when(has_upper)
        def _():
            halo(slot, 1).start()

    def conduct(value, start, count):
        high, low = split(value)
        both = jnp.dot(
            jnp.concatenate([high, low], axis=0), mat_high[start : start + count, :],
            preferred_element_type=jnp.float32,
        )
        rest = jnp.dot(
            high, mat_low[start : start + count, :], preferred_element_type=jnp.float32
        )
        return both[:STEPS] + both[STEPS:] + rest

    real_rows = lax.broadcasted_iota(jnp.int32, (STEPS, 1), 0) <= HALF
    last = coefs[:, 2:3]

    first_own.wait_recv()
    value = jnp.concatenate([psend[group, 0] + pown[0], psend[group, 1] + pown[1]], axis=1)
    total[...] = value
    tail = jnp.sum(value * last, axis=0, keepdims=True)
    result = conduct(value, 0, 8 * BLOCK)

    @pl.when(has_lower)
    def _():
        for sender in range(2):
            first_halo(1, 0, sender).wait_recv()

    result = result + conduct(precv[0, 0] + precv[1, 0], 8 * BLOCK, 4 * BLOCK)

    @pl.when(has_upper)
    def _():
        for sender in range(2):
            first_halo(0, 0, sender).wait_recv()

    result = result + conduct(precv[0, 1] + precv[1, 1], 12 * BLOCK, 4 * BLOCK)
    send(0, divided(result))

    def round_of(slot, tail):
        value = jnp.concatenate([wsend[slot, 0], wsend[slot, 1]], axis=1)
        total[...] += value
        tail = tail + jnp.sum(value * last, axis=0, keepdims=True)
        closes = lax.rem(slot + 1, SWEEPS) == SWEEPS - 1
        fix = jnp.where(closes, tail, 0.0) * capacity[0:1, :]
        tail = jnp.where(closes, 0.0, tail)
        result = conduct(value, 0, 8 * BLOCK) - jnp.where(real_rows, fix, 0.0)

        @pl.when(has_lower)
        def _():
            halo(slot, 1).wait_recv()

        result = result + conduct(wrecv[slot, 0], 8 * BLOCK, 4 * BLOCK)

        @pl.when(has_upper)
        def _():
            halo(slot, 0).wait_recv()

        result = result + conduct(wrecv[slot, 1], 12 * BLOCK, 4 * BLOCK)
        return divided(result), tail

    def step(slot, tail):
        value, tail = round_of(slot, tail)
        send(slot + 1, value)
        return tail

    tail = lax.fori_loop(0, ROUNDS - 2, step, tail)
    value, _ = round_of(ROUNDS - 2, tail)

    places = []
    for block in range(8):
        place = jnp.int32(0)
        for i in range(1, 8):
            place = place + jnp.where(ids[i] == block, i, 0)
        places.append(place)
    summed = product(backward[...], reorder(total[...] + value, places))
    early, late = summed[:HALF], summed[HALF:]
    ysend[...] = jnp.where(first, late, early)
    ycopy = pltpu.make_async_remote_copy(
        src_ref=ysend, dst_ref=yrecv, send_sem=last_sems.at[0], recv_sem=last_sems.at[1],
        device_id=(other, shard), device_id_type=MESH,
    )
    ycopy.start()

    first_own.wait_send()

    @pl.when(has_lower)
    def _():
        for case in range(2):
            first_halo(0, case, group).wait_send()
        for slot in range(ROUNDS - 1):
            halo(slot, 0).wait_send()

    @pl.when(has_upper)
    def _():
        for case in range(2):
            first_halo(1, case, group).wait_send()
        for slot in range(ROUNDS - 1):
            halo(slot, 1).wait_send()

    kept = jnp.where(first, early, late)
    ycopy.wait()
    came = yrecv[...]
    out[:, 0, :] = jnp.where(first, kept, came)
    out[:, 1, :] = jnp.where(first, came, kept)


def per_device(adj_source, terminal, capacity, blocks, columns, face_lists):
    nodes = capacity.shape[0]
    forward, backward, coefs = tables()
    hbm = pl.BlockSpec(memory_space=pltpu.HBM)
    f32, bf16, i32 = jnp.float32, jnp.bfloat16, jnp.int32
    dma = pltpu.SemaphoreType.DMA
    return pl.pallas_call(
        kernel,
        out_shape=jax.ShapeDtypeStruct(adj_source.shape, f32),
        in_specs=[hbm] * 9,
        out_specs=pl.BlockSpec(memory_space=pltpu.VMEM),
        scratch_shapes=[
            pltpu.VMEM(adj_source.shape, f32),
            pltpu.VMEM(terminal.shape, f32),
            pltpu.VMEM((1, nodes), f32),
            pltpu.SMEM(columns.shape, i32),
            pltpu.SMEM(face_lists.shape, i32),
            pltpu.VMEM(forward.shape, bf16),
            pltpu.VMEM(backward.shape, bf16),
            pltpu.VMEM(coefs.shape, f32),
            pltpu.VMEM(blocks.shape, f32),
            pltpu.VMEM((7, BLOCK, LANES), f32),
            pltpu.VMEM((16 * BLOCK, nodes), bf16),
            pltpu.VMEM((16 * BLOCK, nodes), bf16),
            pltpu.VMEM((8, nodes), f32),
            pltpu.VMEM((3, HALF, nodes), f32),
            pltpu.VMEM((8, nodes), f32),
            pltpu.VMEM((2, 2, STEPS, nodes // 2), f32),
            pltpu.VMEM((2, 2, STEPS, nodes // 2), f32),
            pltpu.VMEM((2, STEPS, nodes // 2), f32),
            pltpu.VMEM((ROUNDS - 1, 2, STEPS, nodes // 2), f32),
            pltpu.VMEM((ROUNDS - 1, 2, STEPS, nodes // 2), f32),
            pltpu.VMEM((STEPS, nodes), f32),
            pltpu.VMEM((HALF, nodes), f32),
            pltpu.VMEM((HALF, nodes), f32),
            dma((9,)),
            dma((5,)),
            dma((5,)),
            dma((2,)),
            dma((ROUNDS - 1, 2)),
            dma((ROUNDS - 1, 2)),
        ],
        compiler_params=pltpu.CompilerParams(
            collective_id=0, has_side_effects=True, vmem_limit_bytes=60 * 1024 * 1024
        ),
        name="window",
    )(
        adj_source, terminal, capacity.reshape(1, nodes), columns, face_lists,
        jnp.asarray(forward), jnp.asarray(backward), jnp.asarray(coefs), blocks,
    )


def solution(mesh):
    return jax.shard_map(
        per_device,
        mesh=mesh,
        in_specs=(
            P("tm", None, "space"),
            P(None, "space"),
            P("space"),
            P("space", None, None, None),
            P("space", None),
            P("space", None, None),
        ),
        out_specs=P("tm", None, "space"),
        check_vma=False,
    )
```

```python
import functools
import math

import jax
import jax.numpy as jnp
import numpy as np
from jax import lax
from jax.experimental import pallas as pl
from jax.experimental.pallas import tpu as pltpu
from jax.sharding import PartitionSpec as P

OUTER = 3
SWEEPS = 3
STEPS = 32
HALF = STEPS // 2
CORNER_WEIGHT = 0.1
ROOT = CORNER_WEIGHT ** (1.0 / STEPS)
PAIRS = (OUTER * SWEEPS - 3) // 2
BLOCK = 64
LANES = 128
MESH = pl.DeviceIdType.MESH


def split(value):
    high = value.astype(jnp.bfloat16)
    low = (value - high.astype(jnp.float32)).astype(jnp.bfloat16)
    return high, low


def split_table(table):
    high = table.astype(jnp.bfloat16)
    low = (table - high.astype(np.float64)).astype(jnp.bfloat16)
    return np.concatenate([high, high, low], axis=1)


def tables():
    steps = np.arange(STEPS)
    modes = np.arange(HALF)
    angles = 2.0 * np.pi * ((modes[:, None] * steps[None, :]) % STEPS) / STEPS
    nyquist = (-1.0) ** steps
    cosines, sines = np.cos(angles), -np.sin(angles)
    sines[0] = nyquist
    basis = np.concatenate([cosines, sines], axis=0)
    scale = CORNER_WEIGHT ** (steps / STEPS)
    forward = basis * scale[None, :]
    weight = np.full((STEPS,), 2.0)
    weight[0] = weight[HALF] = 1.0
    inverse = (basis * weight[:, None]).T / STEPS
    last = inverse[STEPS - 1] * ROOT
    backward = inverse / scale[:, None]
    real_coef = 1.0 - ROOT * np.cos(2.0 * np.pi * modes / STEPS)
    imag_coef = ROOT * np.sin(2.0 * np.pi * modes / STEPS)
    real_low = real_coef.copy()
    real_low[0] = 1.0 + ROOT
    columns = np.zeros((STEPS, LANES), np.float32)
    columns[:HALF, 0] = real_coef
    columns[HALF:, 0] = real_low
    columns[:HALF, 1] = imag_coef
    columns[:, 2] = last
    halves = [split_table(forward[:, part * HALF : (part + 1) * HALF]) for part in range(2)]
    return np.stack(halves), split_table(backward), columns


def product(table, value):
    high, low = split(value)
    return jnp.dot(
        table, jnp.concatenate([high, low, high], axis=0), preferred_element_type=jnp.float32
    )


def reorder(value, ids):
    lower_half = lax.broadcasted_iota(jnp.int32, (1, LANES), 1) < BLOCK
    both = []
    for tile in range(4):
        plain = value[:, tile * LANES : (tile + 1) * LANES]
        turned = pltpu.roll(plain, BLOCK, 1)
        both.append(jnp.where(lower_half, plain, turned))
        both.append(jnp.where(lower_half, turned, plain))
    tiles = []
    for tile in range(4):
        wanted = jnp.where(lower_half, ids[2 * tile], ids[2 * tile + 1])
        total = both[0]
        for block in range(1, 8):
            total = jnp.where(wanted == block, both[block], total)
        tiles.append(total)
    return jnp.concatenate(tiles, axis=1)


def kernel(
    adj_hbm, term_hbm, cap_hbm, cols_hbm, faces_hbm, forward_hbm, backward_hbm, coefs_hbm,
    blocks_hbm, out,
    adj, term, cap, cols, faces, forward, backward, coefs, blk,
    turned, names, mat_high, mat_low, face_high, face_low, diag, recip, face_recip, capacity,
    meta, met, tiles, psend, precv, pown, wsend, near, far, own_part, part, total, ysend, yrecv,
    load_sems, first_send, first_recv, once_send, once_recv, last_sems, send_sems, recv_sems,
):
    group = lax.axis_index("tm")
    shard = lax.axis_index("space")
    shards = lax.axis_size("space")
    other = 1 - group
    first = group == 0
    has = (shard > 0, shard < shards - 1)
    has_far = (shard > 1, shard < shards - 2)
    beside = (jnp.maximum(shard - 1, 0), jnp.minimum(shard + 1, shards - 1))
    beyond = (jnp.maximum(shard - 2, 0), jnp.minimum(shard + 2, shards - 1))

    barrier = pltpu.get_barrier_semaphore()

    def greet(target):
        pl.semaphore_signal(barrier, inc=1, device_id=target, device_id_type=MESH)

    greets = 1
    for side in range(2):

        @pl.when(has_far[side])
        def _():
            greet((group, beyond[side]))

        @pl.when(has[side])
        def _():
            greet((0, beside[side]))
            greet((1, beside[side]))

        greets = greets + 2 * has[side].astype(jnp.int32) + has_far[side].astype(jnp.int32)

    greet((other, shard))

    loads = [
        pltpu.make_async_copy(source, target, load_sems.at[i])
        for i, (source, target) in enumerate(
            [
                (faces_hbm, faces), (cols_hbm, cols), (adj_hbm, adj), (term_hbm, term),
                (cap_hbm, cap), (coefs_hbm, coefs), (forward_hbm, forward),
                (blocks_hbm, blk), (backward_hbm, backward),
            ]
        )
    ]
    for load in loads:
        load.start()

    for side in range(2):

        @pl.when(jnp.logical_not(has_far[side]))
        def _():
            far[:, side] = jnp.zeros_like(far[:, side])

        @pl.when(jnp.logical_not(has[side]))
        def _():
            near[:, side] = jnp.zeros_like(near[:, side])
            part[:, side] = jnp.zeros_like(part[:, side])
            precv[:, side] = jnp.zeros_like(precv[:, side])
            tiles[side] = jnp.zeros_like(tiles[side])
            met[side] = jnp.ones_like(met[side])

    for load in loads:
        load.wait()

    ids = [faces[0, i // 4, i % 4] for i in range(8)]
    cap_row = cap[...]
    capacity[...] = reorder(jnp.broadcast_to(cap_row, (8, 8 * BLOCK)), ids)
    eye = lax.broadcasted_iota(jnp.int32, (BLOCK, BLOCK), 0) == lax.broadcasted_iota(
        jnp.int32, (BLOCK, BLOCK), 1
    )
    rows = [
        jnp.sum(jnp.where(eye, blk[ids[i], 0], 0.0), axis=0, keepdims=True) for i in range(8)
    ]
    diag[...] = jnp.broadcast_to(jnp.concatenate(rows, axis=1), diag.shape)

    def reciprocals(cap_own, diag_own):
        imag = coefs[0:HALF, 1:2] * cap_own
        found = []
        for half in range(2):
            real = coefs[half * HALF : (half + 1) * HALF, 0:1] * cap_own + diag_own
            over = 1.0 / (real * real + imag * imag)
            found.append(real * over)
            if half == 0:
                turn = -imag * over
        return found[0], found[1], turn

    def divide(value, upper_real, lower_real, turn):
        upper_part, lower_part = value[:HALF], value[HALF:]
        return jnp.concatenate(
            [
                upper_real * upper_part - turn * lower_part,
                turn * upper_part + lower_real * lower_part,
            ],
            axis=0,
        )

    recip[0], recip[1], recip[2] = reciprocals(capacity[0:1, :], diag[0:1, :])

    def divided(value):
        return divide(value, recip[0], recip[1], recip[2])

    head_row = first & (lax.broadcasted_iota(jnp.int32, (HALF, 1), 0) == 0)
    for case in range(2):
        source = adj[:, case, :] + jnp.where(head_row, term[case : case + 1, :] * cap_row, 0.0)
        field = divided(reorder(product(forward[group], source), ids))
        psend[case, 0] = field[:, : 4 * BLOCK]
        psend[case, 1] = field[:, 4 * BLOCK :]

    lower_half = lax.broadcasted_iota(jnp.int32, (1, LANES), 1) < BLOCK
    turned_eye = lax.broadcasted_iota(jnp.int32, (BLOCK, LANES), 0) == lax.rem(
        lax.broadcasted_iota(jnp.int32, (BLOCK, LANES), 1), BLOCK
    )
    for pair in range(4):
        left, right = ids[2 * pair], ids[2 * pair + 1]
        for k in range(7):
            entry = jnp.concatenate([blk[left, k], blk[right, k]], axis=0)
            entry = -entry.T
            if k == 0:
                entry = jnp.where(turned_eye, 0.0, entry)
            turned[pair, k] = entry
            names[8 * pair + k : 8 * pair + k + 1, :] = jnp.where(
                lower_half, cols[left, k], cols[right, k]
            )
        names[8 * pair + 7 : 8 * pair + 8, :] = jnp.full((1, LANES), -1, jnp.int32)
    raw = names[...]
    place_of = jnp.zeros_like(raw)
    for i in range(8):
        place_of = jnp.where(raw == ids[i], i, place_of)
    place_of = jnp.where(raw >= 8, jnp.where(has[0], raw, -1), place_of)
    place_of = jnp.where(raw >= 12, jnp.where(has[1], raw, -1), place_of)
    named = place_of.astype(jnp.float32)
    for side in range(2):
        meta[side, 0:16] = named[16 * side : 16 * side + 16]
        for row, table in ((16, capacity), (24, diag)):
            for pair in range(2):
                lane = (2 * side + pair) * LANES
                meta[side, row + 4 * pair : row + 4 * pair + 4] = table[0:4, lane : lane + LANES]
    for pair in range(4):
        wanted = [named[8 * pair + k : 8 * pair + k + 1] for k in range(7)]

        def build(place, carry, pair=pair, wanted=wanted):
            name = place.astype(jnp.float32)
            tile = jnp.where(wanted[0] == name, turned[pair, 0], 0.0)
            for k in range(1, 7):
                tile = tile + jnp.where(wanted[k] == name, turned[pair, k], 0.0)
            high, low = split(tile)
            at = pl.ds(pl.multiple_of(place * BLOCK, BLOCK), BLOCK)
            mat_high[at, pair * LANES : (pair + 1) * LANES] = high
            mat_low[at, pair * LANES : (pair + 1) * LANES] = low
            return carry

        lax.fori_loop(0, 16, build, 0)

    pl.semaphore_wait(barrier, greets)

    def remote(source, target, send_sem, recv_sem, device):
        return pltpu.make_async_remote_copy(
            src_ref=source, dst_ref=target, send_sem=send_sem, recv_sem=recv_sem,
            device_id=device, device_id_type=MESH,
        )

    def first_halo(side, case, sender):
        return remote(
            psend.at[case, side], precv.at[sender, 1 - side],
            first_send.at[2 * side + case], first_recv.at[2 * (1 - side) + sender],
            (case, beside[side]),
        )

    first_own = remote(
        psend.at[other], pown, first_send.at[4], first_recv.at[4], (other, shard)
    )

    def matrix_rows(side):
        return remote(
            turned.at[2 * side + group, pl.ds(1, 6)], tiles.at[1 - side, group],
            once_send.at[side], once_recv.at[1 - side], (group, beside[side]),
        )

    def row_facts(side):
        return remote(
            meta.at[side], met.at[1 - side],
            once_send.at[2 + side], once_recv.at[3 - side], (group, beside[side]),
        )

    def passed_on(side):
        return remote(
            tiles.at[side, group], tiles.at[side, group],
            once_send.at[4 + side], once_recv.at[4 + side], (other, shard),
        )

    def field_near(slot, side):
        return remote(
            wsend.at[slot, side], near.at[slot, 1 - side],
            send_sems.at[slot, side], recv_sems.at[slot, 1 - side], (group, beside[side]),
        )

    def field_far(slot, side):
        return remote(
            wsend.at[slot, side], far.at[slot, 1 - side],
            send_sems.at[slot, 2 + side], recv_sems.at[slot, 3 - side], (group, beyond[side]),
        )

    def part_near(slot, side):
        return remote(
            own_part.at[slot, side], part.at[slot, 1 - side],
            send_sems.at[slot, 4 + side], recv_sems.at[slot, 5 - side], (group, beside[side]),
        )

    for side in range(2):

        @pl.when(has[side])
        def _():
            for case in range(2):
                first_halo(side, case, group).start()

    first_own.start()
    for side in range(2):

        @pl.when(has[side])
        def _():
            row_facts(side).start()
            matrix_rows(side).start()

    def times(value, matrix_high, matrix_low):
        high, low = split(value)
        both = jnp.dot(
            jnp.concatenate([high, low], axis=0), matrix_high, preferred_element_type=jnp.float32
        )
        rest = jnp.dot(high, matrix_low, preferred_element_type=jnp.float32)
        return both[:STEPS] + both[STEPS:] + rest

    def conduct(value, start, count):
        return times(
            value, mat_high[start : start + count, :], mat_low[start : start + count, :]
        )

    def face(value, side, start):
        return times(
            value, face_high[side, start : start + 4 * BLOCK], face_low[side, start : start + 4 * BLOCK]
        )

    real_rows = lax.broadcasted_iota(jnp.int32, (STEPS, 1), 0) <= HALF
    last = coefs[:, 2:3]

    def own_product(value, tail, application):
        total[...] += value
        tail = tail + jnp.sum(value * last, axis=0, keepdims=True)
        closes = lax.rem(application, SWEEPS) == SWEEPS - 1
        fix = jnp.where(closes, tail, 0.0) * capacity[0:1, :]
        tail = jnp.where(closes, 0.0, tail)
        return conduct(value, 0, 8 * BLOCK) - jnp.where(real_rows, fix, 0.0), tail

    def advance(slot, value, tail):
        wsend[slot, 0] = value[:, : 4 * BLOCK]
        wsend[slot, 1] = value[:, 4 * BLOCK :]
        paired = slot < PAIRS
        for side in range(2):

            @pl.when(has_far[side] & paired)
            def _():
                field_far(slot, side).start()

        for side in range(2):

            @pl.when(has[side])
            def _():
                field_near(slot, side).start()

        result, tail = own_product(value, tail, 2 * slot + 1)
        own_part[slot, 0] = result[:, : 4 * BLOCK]
        own_part[slot, 1] = result[:, 4 * BLOCK :]
        for side in range(2):

            @pl.when(has[side] & paired)
            def _():
                part_near(slot, side).start()

        return tail

    first_own.wait_recv()
    value = jnp.concatenate([psend[group, 0] + pown[0], psend[group, 1] + pown[1]], axis=1)
    total[...] = jnp.zeros_like(total)
    result, tail = own_product(value, jnp.zeros((1, 8 * BLOCK), jnp.float32), jnp.int32(0))
    for side in range(2):

        @pl.when(has[side])
        def _():
            for sender in range(2):
                first_halo(1 - side, 0, sender).wait_recv()

        result = result + conduct(
            precv[0, side] + precv[1, side], (8 + 4 * side) * BLOCK, 4 * BLOCK
        )
    tail = advance(jnp.int32(0), divided(result), tail)

    for side in range(2):

        @pl.when(has[side])
        def _():
            matrix_rows(1 - side).wait_recv()
            passed_on(side).start()

    for side in range(2):

        @pl.when(has[side])
        def _():
            row_facts(1 - side).wait_recv()

        face_recip[side, 0], face_recip[side, 1], face_recip[side, 2] = reciprocals(
            jnp.concatenate([met[side, 16:17], met[side, 20:21]], axis=1),
            jnp.concatenate([met[side, 24:25], met[side, 28:29]], axis=1),
        )

        @pl.when(has[side])
        def _():
            passed_on(side).wait_recv()

        for pair in range(2):

            def build(place, carry, side=side, pair=pair):
                name = (place + 8).astype(jnp.float32)
                tile = jnp.where(
                    met[side, 8 * pair + 1 : 8 * pair + 2] == name, tiles[side, pair, 0], 0.0
                )
                for k in range(2, 7):
                    wanted = met[side, 8 * pair + k : 8 * pair + k + 1]
                    tile = tile + jnp.where(wanted == name, tiles[side, pair, k - 1], 0.0)
                high, low = split(tile)
                at = pl.ds(pl.multiple_of(place * BLOCK, BLOCK), BLOCK)
                face_high[side, at, pair * LANES : (pair + 1) * LANES] = high
                face_low[side, at, pair * LANES : (pair + 1) * LANES] = low
                return carry

            lax.fori_loop(0, 8, build, 0)

    def couple(slot, tail):
        faces_of = [face(wsend[slot, side], side, 4 * (1 - side) * BLOCK) for side in range(2)]
        result = jnp.concatenate([own_part[slot, 0], own_part[slot, 1]], axis=1)
        for side in range(2):

            @pl.when(has[side])
            def _():
                field_near(slot, 1 - side).wait_recv()

            result = result + conduct(near[slot, side], (8 + 4 * side) * BLOCK, 4 * BLOCK)
        result, tail = own_product(divided(result), tail, 2 * slot + 2)
        for side in range(2):

            @pl.when(has_far[side])
            def _():
                field_far(slot, 1 - side).wait_recv()

            ahead = faces_of[side] + face(far[slot, side], side, 4 * side * BLOCK)

            @pl.when(has[side])
            def _():
                part_near(slot, 1 - side).wait_recv()

            ahead = divide(
                ahead + part[slot, side],
                face_recip[side, 0], face_recip[side, 1], face_recip[side, 2],
            )
            result = result + conduct(ahead, (8 + 4 * side) * BLOCK, 4 * BLOCK)
        return advance(slot + 1, divided(result), tail)

    lax.fori_loop(0, PAIRS, couple, tail)

    result = jnp.concatenate([own_part[PAIRS, 0], own_part[PAIRS, 1]], axis=1)
    for side in range(2):

        @pl.when(has[side])
        def _():
            field_near(PAIRS, 1 - side).wait_recv()

        result = result + conduct(near[PAIRS, side], (8 + 4 * side) * BLOCK, 4 * BLOCK)
    value = divided(result)

    places = []
    for block in range(8):
        place = jnp.int32(0)
        for i in range(1, 8):
            place = place + jnp.where(ids[i] == block, i, 0)
        places.append(place)
    summed = product(backward[...], reorder(total[...] + value, places))
    early, late = summed[:HALF], summed[HALF:]
    ysend[...] = jnp.where(first, late, early)
    ycopy = remote(ysend, yrecv, last_sems.at[0], last_sems.at[1], (other, shard))
    ycopy.start()

    first_own.wait_send()
    for side in range(2):

        @pl.when(has[side])
        def _():
            for case in range(2):
                first_halo(side, case, group).wait_send()
            matrix_rows(side).wait_send()
            row_facts(side).wait_send()
            passed_on(side).wait_send()
            for slot in range(PAIRS + 1):
                field_near(slot, side).wait_send()
            for slot in range(PAIRS):
                part_near(slot, side).wait_send()

        @pl.when(has_far[side])
        def _():
            for slot in range(PAIRS):
                field_far(slot, side).wait_send()

    kept = jnp.where(first, early, late)
    ycopy.wait()
    came = yrecv[...]
    out[:, 0, :] = jnp.where(first, kept, came)
    out[:, 1, :] = jnp.where(first, came, kept)


def per_device(adj_source, terminal, capacity, blocks, columns, face_lists):
    nodes = capacity.shape[0]
    half = nodes // 2
    forward, backward, coefs = tables()
    hbm = pl.BlockSpec(memory_space=pltpu.HBM)
    f32, bf16, i32 = jnp.float32, jnp.bfloat16, jnp.int32
    dma = pltpu.SemaphoreType.DMA
    return pl.pallas_call(
        kernel,
        out_shape=pltpu.VMEM(adj_source.shape, f32),
        in_specs=[hbm] * 9,
        out_specs=pl.BlockSpec(memory_space=pltpu.VMEM),
        scratch_shapes=[
            pltpu.VMEM(adj_source.shape, f32),
            pltpu.VMEM(terminal.shape, f32),
            pltpu.VMEM((1, nodes), f32),
            pltpu.SMEM(columns.shape, i32),
            pltpu.SMEM(face_lists.shape, i32),
            pltpu.VMEM(forward.shape, bf16),
            pltpu.VMEM(backward.shape, bf16),
            pltpu.VMEM(coefs.shape, f32),
            pltpu.VMEM(blocks.shape, f32),
            pltpu.VMEM((4, 7, BLOCK, LANES), f32),
            pltpu.VMEM((32, LANES), i32),
            pltpu.VMEM((16 * BLOCK, nodes), bf16),
            pltpu.VMEM((16 * BLOCK, nodes), bf16),
            pltpu.VMEM((2, 8 * BLOCK, half), bf16),
            pltpu.VMEM((2, 8 * BLOCK, half), bf16),
            pltpu.VMEM((8, nodes), f32),
            pltpu.VMEM((3, HALF, nodes), f32),
            pltpu.VMEM((2, 3, HALF, half), f32),
            pltpu.VMEM((8, nodes), f32),
            pltpu.VMEM((2, 32, LANES), f32),
            pltpu.VMEM((2, 32, LANES), f32),
            pltpu.VMEM((2, 2, 6, BLOCK, LANES), f32),
            pltpu.VMEM((2, 2, STEPS, half), f32),
            pltpu.VMEM((2, 2, STEPS, half), f32),
            pltpu.VMEM((2, STEPS, half), f32),
            pltpu.VMEM((PAIRS + 1, 2, STEPS, half), f32),
            pltpu.VMEM((PAIRS + 1, 2, STEPS, half), f32),
            pltpu.VMEM((PAIRS + 1, 2, STEPS, half), f32),
            pltpu.VMEM((PAIRS + 1, 2, STEPS, half), f32),
            pltpu.VMEM((PAIRS + 1, 2, STEPS, half), f32),
            pltpu.VMEM((STEPS, nodes), f32),
            pltpu.VMEM((HALF, nodes), f32),
            pltpu.VMEM((HALF, nodes), f32),
            dma((9,)),
            dma((5,)),
            dma((5,)),
            dma((6,)),
            dma((6,)),
            dma((2,)),
            dma((PAIRS + 1, 6)),
            dma((PAIRS + 1, 6)),
        ],
        compiler_params=pltpu.CompilerParams(
            collective_id=0, has_side_effects=True, vmem_limit_bytes=60 * 1024 * 1024
        ),
        name="window",
    )(
        adj_source, terminal, capacity.reshape(1, nodes), columns, face_lists,
        jnp.asarray(forward), jnp.asarray(backward), jnp.asarray(coefs), blocks,
    )


def solution(mesh):
    return jax.shard_map(
        per_device,
        mesh=mesh,
        in_specs=(
            P("tm", None, "space"),
            P(None, "space"),
            P("space"),
            P("space", None, None, None),
            P("space", None),
            P("space", None, None),
        ),
        out_specs=P("tm", None, "space"),
        check_vma=False,
    )
```

```python
import functools
import math

import jax
import jax.numpy as jnp
import numpy as np
from jax import lax
from jax.experimental import pallas as pl
from jax.experimental.pallas import tpu as pltpu
from jax.sharding import PartitionSpec as P

OUTER = 3
SWEEPS = 3
STEPS = 32
HALF = STEPS // 2
CORNER_WEIGHT = 0.1
ROOT = CORNER_WEIGHT ** (1.0 / STEPS)
PAIRS = (OUTER * SWEEPS - 3) // 2
BLOCK = 64
LANES = 128
MESH = pl.DeviceIdType.MESH


def split(value):
    high = value.astype(jnp.bfloat16)
    low = (value - high.astype(jnp.float32)).astype(jnp.bfloat16)
    return high, low


def split_table(table):
    high = table.astype(jnp.bfloat16)
    low = (table - high.astype(np.float64)).astype(jnp.bfloat16)
    return np.concatenate([high, high, low], axis=1)


def tables():
    steps = np.arange(STEPS)
    modes = np.arange(HALF)
    angles = 2.0 * np.pi * ((modes[:, None] * steps[None, :]) % STEPS) / STEPS
    nyquist = (-1.0) ** steps
    cosines, sines = np.cos(angles), -np.sin(angles)
    sines[0] = nyquist
    basis = np.concatenate([cosines, sines], axis=0)
    scale = CORNER_WEIGHT ** (steps / STEPS)
    forward = basis * scale[None, :]
    weight = np.full((STEPS,), 2.0)
    weight[0] = weight[HALF] = 1.0
    inverse = (basis * weight[:, None]).T / STEPS
    last = inverse[STEPS - 1] * ROOT
    backward = inverse / scale[:, None]
    real_coef = 1.0 - ROOT * np.cos(2.0 * np.pi * modes / STEPS)
    imag_coef = ROOT * np.sin(2.0 * np.pi * modes / STEPS)
    real_low = real_coef.copy()
    real_low[0] = 1.0 + ROOT
    columns = np.zeros((STEPS, LANES), np.float32)
    columns[:HALF, 0] = real_coef
    columns[HALF:, 0] = real_low
    columns[:HALF, 1] = imag_coef
    columns[:, 2] = last
    halves = [split_table(forward[:, part * HALF : (part + 1) * HALF]) for part in range(2)]
    return np.stack(halves), split_table(backward), columns


def product(table, value):
    high, low = split(value)
    return jnp.dot(
        table, jnp.concatenate([high, low, high], axis=0), preferred_element_type=jnp.float32
    )


def reorder(value, ids):
    lower_half = lax.broadcasted_iota(jnp.int32, (1, LANES), 1) < BLOCK
    both = []
    for tile in range(4):
        plain = value[:, tile * LANES : (tile + 1) * LANES]
        turned = pltpu.roll(plain, BLOCK, 1)
        both.append(jnp.where(lower_half, plain, turned))
        both.append(jnp.where(lower_half, turned, plain))
    tiles = []
    for tile in range(4):
        wanted = jnp.where(lower_half, ids[2 * tile], ids[2 * tile + 1])
        total = both[0]
        for block in range(1, 8):
            total = jnp.where(wanted == block, both[block], total)
        tiles.append(total)
    return jnp.concatenate(tiles, axis=1)


def kernel(
    adj_hbm, term_hbm, cap_hbm, cols_hbm, faces_hbm, forward_hbm, backward_hbm, coefs_hbm,
    blocks_hbm, out,
    adj, term, cap, cols, faces, forward, backward, coefs, blk,
    turned, names, mat_high, mat_low, face_high, face_low, diag, recip, face_recip, capacity,
    meta, met, tiles, psend, precv, pown, wsend, near, far, own_part, part_send, part, total, ysend, yrecv,
    load_sems, first_send, first_recv, once_send, once_recv, last_sems, send_sems, recv_sems,
):
    group = lax.axis_index("tm")
    shard = lax.axis_index("space")
    shards = lax.axis_size("space")
    other = 1 - group
    first = group == 0
    has = (shard > 0, shard < shards - 1)
    has_far = (shard > 1, shard < shards - 2)
    beside = (jnp.maximum(shard - 1, 0), jnp.minimum(shard + 1, shards - 1))
    beyond = (jnp.maximum(shard - 2, 0), jnp.minimum(shard + 2, shards - 1))

    barrier = pltpu.get_barrier_semaphore()

    def greet(target):
        pl.semaphore_signal(barrier, inc=1, device_id=target, device_id_type=MESH)

    greets = 1
    for side in range(2):

        @pl.when(has_far[side])
        def _():
            greet((group, beyond[side]))

        @pl.when(has[side])
        def _():
            greet((0, beside[side]))
            greet((1, beside[side]))

        greets = greets + 2 * has[side].astype(jnp.int32) + has_far[side].astype(jnp.int32)

    greet((other, shard))

    loads = [
        pltpu.make_async_copy(source, target, load_sems.at[i])
        for i, (source, target) in enumerate(
            [
                (faces_hbm, faces), (cols_hbm, cols), (adj_hbm, adj), (term_hbm, term),
                (cap_hbm, cap), (coefs_hbm, coefs), (forward_hbm, forward),
                (blocks_hbm, blk), (backward_hbm, backward),
            ]
        )
    ]
    for load in loads:
        load.start()

    for side in range(2):

        @pl.when(jnp.logical_not(has_far[side]))
        def _():
            far[:, side] = jnp.zeros_like(far[:, side])

        @pl.when(jnp.logical_not(has[side]))
        def _():
            near[:, side] = jnp.zeros_like(near[:, side])
            part[:, side] = jnp.zeros_like(part[:, side])
            precv[:, side] = jnp.zeros_like(precv[:, side])
            tiles[side] = jnp.zeros_like(tiles[side])
            met[side] = jnp.ones_like(met[side])

    for load in loads:
        load.wait()

    ids = [faces[0, i // 4, i % 4] for i in range(8)]
    cap_row = cap[...]
    capacity[...] = reorder(jnp.broadcast_to(cap_row, (8, 8 * BLOCK)), ids)
    eye = lax.broadcasted_iota(jnp.int32, (BLOCK, BLOCK), 0) == lax.broadcasted_iota(
        jnp.int32, (BLOCK, BLOCK), 1
    )
    rows = [
        jnp.sum(jnp.where(eye, blk[ids[i], 0], 0.0), axis=0, keepdims=True) for i in range(8)
    ]
    diag[...] = jnp.broadcast_to(jnp.concatenate(rows, axis=1), diag.shape)

    def reciprocals(cap_own, diag_own):
        imag = coefs[0:HALF, 1:2] * cap_own
        found = []
        for half in range(2):
            real = coefs[half * HALF : (half + 1) * HALF, 0:1] * cap_own + diag_own
            over = 1.0 / (real * real + imag * imag)
            found.append(real * over)
            if half == 0:
                turn = -imag * over
        return found[0], found[1], turn

    def divide(value, upper_real, lower_real, turn):
        upper_part, lower_part = value[:HALF], value[HALF:]
        return jnp.concatenate(
            [
                upper_real * upper_part - turn * lower_part,
                turn * upper_part + lower_real * lower_part,
            ],
            axis=0,
        )

    recip[0], recip[1], recip[2] = reciprocals(capacity[0:1, :], diag[0:1, :])

    def divided(value):
        return divide(value, recip[0], recip[1], recip[2])

    head_row = first & (lax.broadcasted_iota(jnp.int32, (HALF, 1), 0) == 0)
    for case in range(2):
        source = adj[:, case, :] + jnp.where(head_row, term[case : case + 1, :] * cap_row, 0.0)
        field = divided(reorder(product(forward[group], source), ids))
        psend[case, 0] = field[:, : 4 * BLOCK]
        psend[case, 1] = field[:, 4 * BLOCK :]

    lower_half = lax.broadcasted_iota(jnp.int32, (1, LANES), 1) < BLOCK
    turned_eye = lax.broadcasted_iota(jnp.int32, (BLOCK, LANES), 0) == lax.rem(
        lax.broadcasted_iota(jnp.int32, (BLOCK, LANES), 1), BLOCK
    )
    for pair in range(4):
        left, right = ids[2 * pair], ids[2 * pair + 1]
        for k in range(7):
            entry = jnp.concatenate([blk[left, k], blk[right, k]], axis=0)
            entry = -entry.T
            if k == 0:
                entry = jnp.where(turned_eye, 0.0, entry)
            turned[pair, k] = entry
            names[8 * pair + k : 8 * pair + k + 1, :] = jnp.where(
                lower_half, cols[left, k], cols[right, k]
            )
        names[8 * pair + 7 : 8 * pair + 8, :] = jnp.full((1, LANES), -1, jnp.int32)
    raw = names[...]
    place_of = jnp.zeros_like(raw)
    for i in range(8):
        place_of = jnp.where(raw == ids[i], i, place_of)
    place_of = jnp.where(raw >= 8, jnp.where(has[0], raw, -1), place_of)
    place_of = jnp.where(raw >= 12, jnp.where(has[1], raw, -1), place_of)
    named = place_of.astype(jnp.float32)
    for side in range(2):
        meta[side, 0:16] = named[16 * side : 16 * side + 16]
        for row, table in ((16, capacity), (24, diag)):
            for pair in range(2):
                lane = (2 * side + pair) * LANES
                meta[side, row + 4 * pair : row + 4 * pair + 4] = table[0:4, lane : lane + LANES]
    for pair in range(4):
        wanted = [named[8 * pair + k : 8 * pair + k + 1] for k in range(7)]

        def build(place, carry, pair=pair, wanted=wanted):
            name = place.astype(jnp.float32)
            tile = jnp.where(wanted[0] == name, turned[pair, 0], 0.0)
            for k in range(1, 7):
                tile = tile + jnp.where(wanted[k] == name, turned[pair, k], 0.0)
            high, low = split(tile)
            at = pl.ds(pl.multiple_of(place * BLOCK, BLOCK), BLOCK)
            mat_high[at, pair * LANES : (pair + 1) * LANES] = high
            mat_low[at, pair * LANES : (pair + 1) * LANES] = low
            return carry

        lax.fori_loop(0, 16, build, 0)

    pl.semaphore_wait(barrier, greets)

    def remote(source, target, send_sem, recv_sem, device):
        return pltpu.make_async_remote_copy(
            src_ref=source, dst_ref=target, send_sem=send_sem, recv_sem=recv_sem,
            device_id=device, device_id_type=MESH,
        )

    def first_halo(side, case, sender):
        return remote(
            psend.at[case, side], precv.at[sender, 1 - side],
            first_send.at[2 * side + case], first_recv.at[2 * (1 - side) + sender],
            (case, beside[side]),
        )

    first_own = remote(
        psend.at[other], pown, first_send.at[4], first_recv.at[4], (other, shard)
    )

    def matrix_rows(side):
        return remote(
            turned.at[2 * side + group, pl.ds(1, 6)], tiles.at[1 - side, group],
            once_send.at[side], once_recv.at[1 - side], (group, beside[side]),
        )

    def row_facts(side):
        return remote(
            meta.at[side], met.at[1 - side],
            once_send.at[2 + side], once_recv.at[3 - side], (group, beside[side]),
        )

    def passed_on(side):
        return remote(
            tiles.at[side, group], tiles.at[side, group],
            once_send.at[4 + side], once_recv.at[4 + side], (other, shard),
        )

    def field_near(slot, side):
        return remote(
            wsend.at[slot, side], near.at[slot, 1 - side],
            send_sems.at[slot, side], recv_sems.at[slot, 1 - side], (group, beside[side]),
        )

    def field_far(slot, side):
        return remote(
            wsend.at[slot, side], far.at[slot, 1 - side],
            send_sems.at[slot, 2 + side], recv_sems.at[slot, 3 - side], (group, beyond[side]),
        )

    def part_near(slot, side):
        return remote(
            part_send.at[slot, side], part.at[slot, 1 - side],
            send_sems.at[slot, 4 + side], recv_sems.at[slot, 5 - side], (group, beside[side]),
        )

    for side in range(2):

        @pl.when(has[side])
        def _():
            for case in range(2):
                first_halo(side, case, group).start()

    first_own.start()

    def times(value, matrix_high, matrix_low):
        high, low = split(value)
        both = jnp.dot(
            jnp.concatenate([high, low], axis=0), matrix_high, preferred_element_type=jnp.float32
        )
        rest = jnp.dot(high, matrix_low, preferred_element_type=jnp.float32)
        return both[:STEPS] + both[STEPS:] + rest

    def conduct(value, start, count):
        return times(
            value, mat_high[start : start + count, :], mat_low[start : start + count, :]
        )

    def received(from_lower, from_upper):
        return conduct(jnp.concatenate([from_lower, from_upper], axis=1), 8 * BLOCK, 8 * BLOCK)

    def face(value, side, start):
        return times(
            value, face_high[side, start : start + 4 * BLOCK], face_low[side, start : start + 4 * BLOCK]
        )

    real_rows = lax.broadcasted_iota(jnp.int32, (STEPS, 1), 0) <= HALF
    last = coefs[:, 2:3]

    def own_product(value, tail, application):
        total[...] += value
        tail = tail + jnp.sum(value * last, axis=0, keepdims=True)
        closes = lax.rem(application, SWEEPS) == SWEEPS - 1
        fix = jnp.where(closes, tail, 0.0) * capacity[0:1, :]
        tail = jnp.where(closes, 0.0, tail)
        return conduct(value, 0, 8 * BLOCK) - jnp.where(real_rows, fix, 0.0), tail

    def advance(slot, value, tail, application, paired):
        wsend[slot, 0] = value[:, : 4 * BLOCK]
        wsend[slot, 1] = value[:, 4 * BLOCK :]
        for side in range(2):

            @pl.when(has[side])
            def _():
                field_near(slot, side).start()

        if paired:
            for side in range(2):

                @pl.when(has_far[side])
                def _():
                    field_far(slot, side).start()

        result, tail = own_product(value, tail, application)
        own_part[slot] = result
        if paired:
            result = divided(result)
            part_send[slot, 0] = result[:, : 4 * BLOCK]
            part_send[slot, 1] = result[:, 4 * BLOCK :]
            for side in range(2):

                @pl.when(has[side])
                def _():
                    part_near(slot, side).start()

        return tail

    def first_step(slot):
        for side in range(2):

            @pl.when(has[side])
            def _():
                field_near(slot, 1 - side).wait_recv()

        return divided(own_part[slot] + received(near[slot, 0], near[slot, 1]))

    first_own.wait_recv()
    value = jnp.concatenate([psend[group, 0] + pown[0], psend[group, 1] + pown[1]], axis=1)
    total[...] = jnp.zeros_like(total)
    result, tail = own_product(value, jnp.zeros((1, 8 * BLOCK), jnp.float32), jnp.int32(0))
    for side in range(2):

        @pl.when(has[side])
        def _():
            row_facts(side).start()
            matrix_rows(side).start()

    for side in range(2):

        @pl.when(has[side])
        def _():
            for sender in range(2):
                first_halo(1 - side, 0, sender).wait_recv()

    result = result + received(precv[0, 0] + precv[1, 0], precv[0, 1] + precv[1, 1])
    tail = advance(0, divided(result), tail, jnp.int32(1), False)

    for side in range(2):

        @pl.when(has[side])
        def _():
            matrix_rows(1 - side).wait_recv()
            passed_on(side).start()

    tail = advance(1, first_step(0), tail, jnp.int32(2), True)

    for side in range(2):

        @pl.when(has[side])
        def _():
            row_facts(1 - side).wait_recv()

        face_recip[side, 0], face_recip[side, 1], face_recip[side, 2] = reciprocals(
            jnp.concatenate([met[side, 16:17], met[side, 20:21]], axis=1),
            jnp.concatenate([met[side, 24:25], met[side, 28:29]], axis=1),
        )

        @pl.when(has[side])
        def _():
            passed_on(side).wait_recv()

        for pair in range(2):

            def build(place, carry, side=side, pair=pair):
                name = (place + 8).astype(jnp.float32)
                tile = jnp.where(
                    met[side, 8 * pair + 1 : 8 * pair + 2] == name, tiles[side, pair, 0], 0.0
                )
                for k in range(2, 7):
                    wanted = met[side, 8 * pair + k : 8 * pair + k + 1]
                    tile = tile + jnp.where(wanted == name, tiles[side, pair, k - 1], 0.0)
                high, low = split(tile)
                at = pl.ds(pl.multiple_of(place * BLOCK, BLOCK), BLOCK)
                face_high[side, at, pair * LANES : (pair + 1) * LANES] = high
                face_low[side, at, pair * LANES : (pair + 1) * LANES] = low
                return carry

            lax.fori_loop(0, 8, build, 0)

    def couple(slot, tail):
        ahead = [face(wsend[slot, side], side, 4 * (1 - side) * BLOCK) for side in range(2)]
        result, tail = own_product(first_step(slot), tail, 2 * slot + 1)
        for side in range(2):

            @pl.when(has_far[side])
            def _():
                field_far(slot, 1 - side).wait_recv()

            ahead[side] = divide(
                ahead[side] + face(far[slot, side], side, 4 * side * BLOCK),
                face_recip[side, 0], face_recip[side, 1], face_recip[side, 2],
            )
        for side in range(2):

            @pl.when(has[side])
            def _():
                part_near(slot, 1 - side).wait_recv()

        result = result + received(ahead[0] + part[slot, 0], ahead[1] + part[slot, 1])
        return divided(result), tail

    def step(slot, tail):
        value, tail = couple(slot, tail)
        return advance(slot + 1, value, tail, 2 * slot + 2, True)

    tail = lax.fori_loop(1, PAIRS, step, tail)
    value, _ = couple(PAIRS, tail)

    places = []
    for block in range(8):
        place = jnp.int32(0)
        for i in range(1, 8):
            place = place + jnp.where(ids[i] == block, i, 0)
        places.append(place)
    summed = product(backward[...], reorder(total[...] + value, places))
    early, late = summed[:HALF], summed[HALF:]
    ysend[...] = jnp.where(first, late, early)
    ycopy = remote(ysend, yrecv, last_sems.at[0], last_sems.at[1], (other, shard))
    ycopy.start()

    first_own.wait_send()
    for side in range(2):

        @pl.when(has[side])
        def _():
            for case in range(2):
                first_halo(side, case, group).wait_send()
            matrix_rows(side).wait_send()
            row_facts(side).wait_send()
            passed_on(side).wait_send()
            for slot in range(PAIRS + 1):
                field_near(slot, side).wait_send()
            for slot in range(1, PAIRS + 1):
                part_near(slot, side).wait_send()

        @pl.when(has_far[side])
        def _():
            for slot in range(1, PAIRS + 1):
                field_far(slot, side).wait_send()

    kept = jnp.where(first, early, late)
    ycopy.wait()
    came = yrecv[...]
    out[:, 0, :] = jnp.where(first, kept, came)
    out[:, 1, :] = jnp.where(first, came, kept)


def per_device(adj_source, terminal, capacity, blocks, columns, face_lists):
    nodes = capacity.shape[0]
    half = nodes // 2
    forward, backward, coefs = tables()
    hbm = pl.BlockSpec(memory_space=pltpu.HBM)
    f32, bf16, i32 = jnp.float32, jnp.bfloat16, jnp.int32
    dma = pltpu.SemaphoreType.DMA
    return pl.pallas_call(
        kernel,
        out_shape=pltpu.VMEM(adj_source.shape, f32),
        in_specs=[hbm] * 9,
        out_specs=pl.BlockSpec(memory_space=pltpu.VMEM),
        scratch_shapes=[
            pltpu.VMEM(adj_source.shape, f32),
            pltpu.VMEM(terminal.shape, f32),
            pltpu.VMEM((1, nodes), f32),
            pltpu.SMEM(columns.shape, i32),
            pltpu.SMEM(face_lists.shape, i32),
            pltpu.VMEM(forward.shape, bf16),
            pltpu.VMEM(backward.shape, bf16),
            pltpu.VMEM(coefs.shape, f32),
            pltpu.VMEM(blocks.shape, f32),
            pltpu.VMEM((4, 7, BLOCK, LANES), f32),
            pltpu.VMEM((32, LANES), i32),
            pltpu.VMEM((16 * BLOCK, nodes), bf16),
            pltpu.VMEM((16 * BLOCK, nodes), bf16),
            pltpu.VMEM((2, 8 * BLOCK, half), bf16),
            pltpu.VMEM((2, 8 * BLOCK, half), bf16),
            pltpu.VMEM((8, nodes), f32),
            pltpu.VMEM((3, HALF, nodes), f32),
            pltpu.VMEM((2, 3, HALF, half), f32),
            pltpu.VMEM((8, nodes), f32),
            pltpu.VMEM((2, 32, LANES), f32),
            pltpu.VMEM((2, 32, LANES), f32),
            pltpu.VMEM((2, 2, 6, BLOCK, LANES), f32),
            pltpu.VMEM((2, 2, STEPS, half), f32),
            pltpu.VMEM((2, 2, STEPS, half), f32),
            pltpu.VMEM((2, STEPS, half), f32),
            pltpu.VMEM((PAIRS + 1, 2, STEPS, half), f32),
            pltpu.VMEM((PAIRS + 1, 2, STEPS, half), f32),
            pltpu.VMEM((PAIRS + 1, 2, STEPS, half), f32),
            pltpu.VMEM((PAIRS + 1, STEPS, nodes), f32),
            pltpu.VMEM((PAIRS + 1, 2, STEPS, half), f32),
            pltpu.VMEM((PAIRS + 1, 2, STEPS, half), f32),
            pltpu.VMEM((STEPS, nodes), f32),
            pltpu.VMEM((HALF, nodes), f32),
            pltpu.VMEM((HALF, nodes), f32),
            dma((9,)),
            dma((5,)),
            dma((5,)),
            dma((6,)),
            dma((6,)),
            dma((2,)),
            dma((PAIRS + 1, 6)),
            dma((PAIRS + 1, 6)),
        ],
        compiler_params=pltpu.CompilerParams(
            collective_id=0, has_side_effects=True, vmem_limit_bytes=60 * 1024 * 1024
        ),
        name="window",
    )(
        adj_source, terminal, capacity.reshape(1, nodes), columns, face_lists,
        jnp.asarray(forward), jnp.asarray(backward), jnp.asarray(coefs), blocks,
    )


def solution(mesh):
    return jax.shard_map(
        per_device,
        mesh=mesh,
        in_specs=(
            P("tm", None, "space"),
            P(None, "space"),
            P("space"),
            P("space", None, None, None),
            P("space", None),
            P("space", None, None),
        ),
        out_specs=P("tm", None, "space"),
        check_vma=False,
    )
```

```python
import functools
import math

import jax
import jax.numpy as jnp
import numpy as np
from jax import lax
from jax.experimental import pallas as pl
from jax.experimental.pallas import tpu as pltpu
from jax.sharding import PartitionSpec as P

OUTER = 3
SWEEPS = 3
STEPS = 32
HALF = STEPS // 2
CORNER_WEIGHT = 0.1
ROOT = CORNER_WEIGHT ** (1.0 / STEPS)
PAIRS = (OUTER * SWEEPS - 3) // 2
BLOCK = 64
LANES = 128
MESH = pl.DeviceIdType.MESH


def split(value):
    high = value.astype(jnp.bfloat16)
    low = (value - high.astype(jnp.float32)).astype(jnp.bfloat16)
    return high, low


def split_table(table):
    high = table.astype(jnp.bfloat16)
    low = (table - high.astype(np.float64)).astype(jnp.bfloat16)
    return np.concatenate([high, high, low], axis=1)


def tables():
    steps = np.arange(STEPS)
    modes = np.arange(HALF)
    angles = 2.0 * np.pi * ((modes[:, None] * steps[None, :]) % STEPS) / STEPS
    nyquist = (-1.0) ** steps
    cosines, sines = np.cos(angles), -np.sin(angles)
    sines[0] = nyquist
    basis = np.concatenate([cosines, sines], axis=0)
    scale = CORNER_WEIGHT ** (steps / STEPS)
    forward = basis * scale[None, :]
    weight = np.full((STEPS,), 2.0)
    weight[0] = weight[HALF] = 1.0
    inverse = (basis * weight[:, None]).T / STEPS
    last = inverse[STEPS - 1] * ROOT
    backward = inverse / scale[:, None]
    real_coef = 1.0 - ROOT * np.cos(2.0 * np.pi * modes / STEPS)
    imag_coef = ROOT * np.sin(2.0 * np.pi * modes / STEPS)
    real_low = real_coef.copy()
    real_low[0] = 1.0 + ROOT
    columns = np.zeros((STEPS, LANES), np.float32)
    columns[:HALF, 0] = real_coef
    columns[HALF:, 0] = real_low
    columns[:HALF, 1] = imag_coef
    columns[:, 2] = last
    halves = [split_table(forward[:, part * HALF : (part + 1) * HALF]) for part in range(2)]
    return np.stack(halves), split_table(backward), columns


def product(table, value):
    high, low = split(value)
    return jnp.dot(
        table, jnp.concatenate([high, low, high], axis=0), preferred_element_type=jnp.float32
    )


def reorder(value, ids):
    lower_half = lax.broadcasted_iota(jnp.int32, (1, LANES), 1) < BLOCK
    both = []
    for tile in range(4):
        plain = value[:, tile * LANES : (tile + 1) * LANES]
        turned = pltpu.roll(plain, BLOCK, 1)
        both.append(jnp.where(lower_half, plain, turned))
        both.append(jnp.where(lower_half, turned, plain))
    tiles = []
    for tile in range(4):
        wanted = jnp.where(lower_half, ids[2 * tile], ids[2 * tile + 1])
        total = both[0]
        for block in range(1, 8):
            total = jnp.where(wanted == block, both[block], total)
        tiles.append(total)
    return jnp.concatenate(tiles, axis=1)


def kernel(
    adj_hbm, term_hbm, cap_hbm, cols_hbm, faces_hbm, forward_hbm, backward_hbm, coefs_hbm,
    blocks_hbm, out,
    adj, term, cap, cols, faces, forward, backward, coefs, blk,
    turned, names, mat_high, mat_low, face_high, face_low, diag, recip, face_recip, capacity,
    meta, met, tiles, psend, precv, pown, wsend, near, far, own_part, part_send, part, middle, tails, total, ysend, yrecv,
    load_sems, first_send, first_recv, once_send, once_recv, last_sems, send_sems, recv_sems,
):
    group = lax.axis_index("tm")
    shard = lax.axis_index("space")
    shards = lax.axis_size("space")
    other = 1 - group
    first = group == 0
    slow = jnp.where(lax.rem(shard, 4) >= 2, 1, 0)
    fast = 1 - slow
    order = (fast, slow)

    def has(side):
        return jnp.where(side == 0, shard > 0, shard < shards - 1)

    def has_far(side):
        return jnp.where(side == 0, shard > 1, shard < shards - 2)

    def beside(side):
        return jnp.clip(shard + 2 * side - 1, 0, shards - 1)

    def beyond(side):
        return jnp.clip(shard + 4 * side - 2, 0, shards - 1)

    barrier = pltpu.get_barrier_semaphore()

    def greet(target):
        pl.semaphore_signal(barrier, inc=1, device_id=target, device_id_type=MESH)

    greets = 1
    for side in range(2):

        @pl.when(has_far(side))
        def _():
            greet((group, beyond(side)))

        @pl.when(has(side))
        def _():
            greet((0, beside(side)))
            greet((1, beside(side)))

        greets = greets + 2 * has(side).astype(jnp.int32) + has_far(side).astype(jnp.int32)

    greet((other, shard))

    loads = [
        pltpu.make_async_copy(source, target, load_sems.at[i])
        for i, (source, target) in enumerate(
            [
                (faces_hbm, faces), (cols_hbm, cols), (adj_hbm, adj), (term_hbm, term),
                (cap_hbm, cap), (coefs_hbm, coefs), (forward_hbm, forward),
                (blocks_hbm, blk), (backward_hbm, backward),
            ]
        )
    ]
    for load in loads:
        load.start()

    for side in range(2):

        @pl.when(jnp.logical_not(has_far(side)))
        def _():
            far[:, side] = jnp.zeros_like(far[:, side])

        @pl.when(jnp.logical_not(has(side)))
        def _():
            near[:, side] = jnp.zeros_like(near[:, side])
            part[:, side] = jnp.zeros_like(part[:, side])
            precv[:, side] = jnp.zeros_like(precv[:, side])
            tiles[side] = jnp.zeros_like(tiles[side])
            met[side] = jnp.ones_like(met[side])

    for load in loads:
        load.wait()

    ids = [faces[0, i // 4, i % 4] for i in range(8)]
    cap_row = cap[...]
    cap_own = reorder(jnp.broadcast_to(cap_row, (8, 8 * BLOCK)), ids)
    eye = lax.broadcasted_iota(jnp.int32, (BLOCK, BLOCK), 0) == lax.broadcasted_iota(
        jnp.int32, (BLOCK, BLOCK), 1
    )
    rows = [
        jnp.sum(jnp.where(eye, blk[ids[i], 0], 0.0), axis=0, keepdims=True) for i in range(8)
    ]
    diag_own = jnp.broadcast_to(jnp.concatenate(rows, axis=1), (8, 8 * BLOCK))
    for half in range(2):
        capacity[half] = cap_own[:, half * 4 * BLOCK : (half + 1) * 4 * BLOCK]
        diag[half] = diag_own[:, half * 4 * BLOCK : (half + 1) * 4 * BLOCK]

    def reciprocals(cap_part, diag_part):
        imag = coefs[0:HALF, 1:2] * cap_part
        found = []
        for half in range(2):
            real = coefs[half * HALF : (half + 1) * HALF, 0:1] * cap_part + diag_part
            over = 1.0 / (real * real + imag * imag)
            found.append(real * over)
            if half == 0:
                turn = -imag * over
        return found[0], found[1], turn

    def divide(value, upper_real, lower_real, turn):
        upper_part, lower_part = value[:HALF], value[HALF:]
        return jnp.concatenate(
            [
                upper_real * upper_part - turn * lower_part,
                turn * upper_part + lower_real * lower_part,
            ],
            axis=0,
        )

    for half in range(2):
        recip[half, 0], recip[half, 1], recip[half, 2] = reciprocals(
            capacity[half, 0:1], diag[half, 0:1]
        )

    def divided(value, half):
        return divide(value, recip[half, 0], recip[half, 1], recip[half, 2])

    head_row = first & (lax.broadcasted_iota(jnp.int32, (HALF, 1), 0) == 0)
    for case in range(2):
        source = adj[:, case, :] + jnp.where(head_row, term[case : case + 1, :] * cap_row, 0.0)
        spectrum = reorder(product(forward[group], source), ids)
        psend[case, 0] = divided(spectrum[:, : 4 * BLOCK], 0)
        psend[case, 1] = divided(spectrum[:, 4 * BLOCK :], 1)

    lower_half = lax.broadcasted_iota(jnp.int32, (1, LANES), 1) < BLOCK
    turned_eye = lax.broadcasted_iota(jnp.int32, (BLOCK, LANES), 0) == lax.rem(
        lax.broadcasted_iota(jnp.int32, (BLOCK, LANES), 1), BLOCK
    )
    for pair in range(4):
        left, right = ids[2 * pair], ids[2 * pair + 1]
        for k in range(7):
            entry = jnp.concatenate([blk[left, k], blk[right, k]], axis=0)
            entry = -entry.T
            if k == 0:
                entry = jnp.where(turned_eye, 0.0, entry)
            turned[pair, k] = entry
            names[8 * pair + k : 8 * pair + k + 1, :] = jnp.where(
                lower_half, cols[left, k], cols[right, k]
            )
        names[8 * pair + 7 : 8 * pair + 8, :] = jnp.full((1, LANES), -1, jnp.int32)
    raw = names[...]
    place_of = jnp.zeros_like(raw)
    for i in range(8):
        place_of = jnp.where(raw == ids[i], i, place_of)
    place_of = jnp.where(raw >= 8, jnp.where(has(0), raw, -1), place_of)
    place_of = jnp.where(raw >= 12, jnp.where(has(1), raw, -1), place_of)
    named = place_of.astype(jnp.float32)
    for side in range(2):
        meta[side, 0:16] = named[16 * side : 16 * side + 16]
        for row, table in ((16, capacity), (24, diag)):
            for pair in range(2):
                meta[side, row + 4 * pair : row + 4 * pair + 4] = table[
                    side, 0:4, pair * LANES : (pair + 1) * LANES
                ]
    for pair in range(4):
        wanted = [named[8 * pair + k : 8 * pair + k + 1] for k in range(7)]

        def build(place, carry, pair=pair, wanted=wanted):
            name = place.astype(jnp.float32)
            tile = jnp.where(wanted[0] == name, turned[pair, 0], 0.0)
            for k in range(1, 7):
                tile = tile + jnp.where(wanted[k] == name, turned[pair, k], 0.0)
            high, low = split(tile)
            at = pl.ds(pl.multiple_of(place * BLOCK, BLOCK), BLOCK)
            lanes = slice(pair % 2 * LANES, (pair % 2 + 1) * LANES)
            mat_high[pair // 2, at, lanes] = high
            mat_low[pair // 2, at, lanes] = low
            return carry

        lax.fori_loop(0, 16, build, 0)

    pl.semaphore_wait(barrier, greets)

    def remote(source, target, send_sem, recv_sem, device):
        return pltpu.make_async_remote_copy(
            src_ref=source, dst_ref=target, send_sem=send_sem, recv_sem=recv_sem,
            device_id=device, device_id_type=MESH,
        )

    def first_halo(side, case, sender):
        return remote(
            psend.at[case, side], precv.at[sender, 1 - side],
            first_send.at[2 * side + case], first_recv.at[2 * (1 - side) + sender],
            (case, beside(side)),
        )

    first_own = remote(
        psend.at[other], pown, first_send.at[4], first_recv.at[4], (other, shard)
    )

    def matrix_rows(side):
        return remote(
            turned.at[2 * side + group, pl.ds(1, 6)], tiles.at[1 - side, group],
            once_send.at[side], once_recv.at[1 - side], (group, beside(side)),
        )

    def row_facts(side):
        return remote(
            meta.at[side], met.at[1 - side],
            once_send.at[2 + side], once_recv.at[3 - side], (group, beside(side)),
        )

    def passed_on(side):
        return remote(
            tiles.at[side, group], tiles.at[side, group],
            once_send.at[4 + side], once_recv.at[4 + side], (other, shard),
        )

    def field_near(slot, side):
        return remote(
            wsend.at[slot, side], near.at[slot, 1 - side],
            send_sems.at[slot, 0, side], recv_sems.at[slot, 0, 1 - side], (group, beside(side)),
        )

    def field_far(slot, side):
        return remote(
            wsend.at[slot, side], far.at[slot, 1 - side],
            send_sems.at[slot, 1, side], recv_sems.at[slot, 1, 1 - side], (group, beyond(side)),
        )

    def part_near(slot, side):
        return remote(
            part_send.at[slot, side], part.at[slot, 1 - side],
            send_sems.at[slot, 2, side], recv_sems.at[slot, 2, 1 - side], (group, beside(side)),
        )

    for side in (slow, fast):

        @pl.when(has(side))
        def _():
            for case in range(2):
                first_halo(side, case, group).start()

    first_own.start()

    def pieces_of(value):
        high, low = split(value)
        return high, jnp.concatenate([high, low], axis=0)

    def times(pieces, matrix_high, matrix_low):
        high, stacked = pieces
        both = jnp.dot(stacked, matrix_high, preferred_element_type=jnp.float32)
        rest = jnp.dot(high, matrix_low, preferred_element_type=jnp.float32)
        return both[:STEPS] + both[STEPS:] + rest

    def rows_of(side):
        return pl.ds(pl.multiple_of(side * (4 * BLOCK), 4 * BLOCK), 4 * BLOCK)

    def received(pieces, half, side):
        rows = rows_of(2 + side)
        return times(pieces, mat_high[half, rows, :], mat_low[half, rows, :])

    def face(value, side, from_side):
        rows = rows_of(from_side)
        return times(pieces_of(value), face_high[side, rows, :], face_low[side, rows, :])

    real_rows = lax.broadcasted_iota(jnp.int32, (STEPS, 1), 0) <= HALF
    last = coefs[:, 2:3]

    def note(value, half):
        total[half] += value
        weighted = value * last
        tails[half] += weighted[0:8] + weighted[8:16] + weighted[16:24] + weighted[24:32]

    def own_product(pieces, half, application):
        closes = lax.rem(application, SWEEPS) == SWEEPS - 1
        tail = jnp.sum(tails[half], axis=0, keepdims=True)
        fix = jnp.where(closes, tail, 0.0) * capacity[half, 0:1]
        tails[half] = jnp.where(closes, 0.0, tails[half])
        result = times(
            pieces, mat_high[half, 0 : 8 * BLOCK, :], mat_low[half, 0 : 8 * BLOCK, :]
        )
        return result - jnp.where(real_rows, fix, 0.0)

    def send_field(slot, side, paired):
        @pl.when(has(side))
        def _():
            field_near(slot, side).start()

        if paired:

            @pl.when(has_far(side))
            def _():
                field_far(slot, side).start()

    def advance(slot, slow_part, fast_part, pieces, application, paired):
        for half, value in ((slow, slow_part), (fast, fast_part)):
            value = divided(value + received(pieces, half, slow), half)
            wsend[slot, half] = value
            send_field(slot, half, paired)
            note(value, half)
        pieces = pieces_of(jnp.concatenate([wsend[slot, 0], wsend[slot, 1]], axis=1))
        for half in (slow, fast):
            result = own_product(pieces, half, application)
            own_part[slot, half] = result
            if paired:
                part_send[slot, half] = divided(result, half)

                @pl.when(has(half))
                def _():
                    part_near(slot, half).start()

    def near_of(slot, side):
        @pl.when(has(side))
        def _():
            field_near(slot, 1 - side).wait_recv()

        return pieces_of(near[slot, side])

    def add_fast(slow_part, fast_part, pieces):
        return slow_part + received(pieces, slow, fast), fast_part + received(pieces, fast, fast)

    def begun(slot):
        return add_fast(own_part[slot, slow], own_part[slot, fast], near_of(slot, fast))

    total[...] = jnp.zeros_like(total)
    tails[...] = jnp.zeros_like(tails)
    first_own.wait_recv()
    halves = [psend[group, half] + pown[half] for half in range(2)]
    for half in range(2):
        note(halves[half], half)
    pieces = pieces_of(jnp.concatenate(halves, axis=1))
    slow_part = own_product(pieces, slow, jnp.int32(0))
    fast_part = own_product(pieces, fast, jnp.int32(0))
    for side in range(2):

        @pl.when(has(side))
        def _():
            row_facts(side).start()
            matrix_rows(side).start()

    for side in order:

        @pl.when(has(side))
        def _():
            for sender in range(2):
                first_halo(1 - side, 0, sender).wait_recv()

        pieces = pieces_of(precv[0, side] + precv[1, side])
        if side is fast:
            slow_part, fast_part = add_fast(slow_part, fast_part, pieces)
    advance(0, slow_part, fast_part, pieces, jnp.int32(1), False)

    for side in range(2):

        @pl.when(has(side))
        def _():
            matrix_rows(1 - side).wait_recv()
            passed_on(side).start()

    advance(1, *begun(0), near_of(0, slow), jnp.int32(2), True)

    for side in range(2):

        @pl.when(has(side))
        def _():
            row_facts(1 - side).wait_recv()

        face_recip[side, 0], face_recip[side, 1], face_recip[side, 2] = reciprocals(
            jnp.concatenate([met[side, 16:17], met[side, 20:21]], axis=1),
            jnp.concatenate([met[side, 24:25], met[side, 28:29]], axis=1),
        )

        @pl.when(has(side))
        def _():
            passed_on(side).wait_recv()

        for pair in range(2):

            def build(place, carry, side=side, pair=pair):
                name = (place + 8).astype(jnp.float32)
                tile = jnp.where(
                    met[side, 8 * pair + 1 : 8 * pair + 2] == name, tiles[side, pair, 0], 0.0
                )
                for k in range(2, 7):
                    wanted = met[side, 8 * pair + k : 8 * pair + k + 1]
                    tile = tile + jnp.where(wanted == name, tiles[side, pair, k - 1], 0.0)
                high, low = split(tile)
                at = pl.ds(pl.multiple_of(place * BLOCK, BLOCK), BLOCK)
                face_high[side, at, pair * LANES : (pair + 1) * LANES] = high
                face_low[side, at, pair * LANES : (pair + 1) * LANES] = low
                return carry

            lax.fori_loop(0, 8, build, 0)

    def ahead_of(slot, side, early):
        @pl.when(has_far(side))
        def _():
            field_far(slot, 1 - side).wait_recv()

        found = divide(
            early + face(far[slot, side], side, side),
            face_recip[side, 0], face_recip[side, 1], face_recip[side, 2],
        )

        @pl.when(has(side))
        def _():
            part_near(slot, 1 - side).wait_recv()

        return pieces_of(found + part[slot, side])

    def couple(slot):
        early = [face(wsend[slot, side], side, 1 - side) for side in order]
        slow_part, fast_part = begun(slot)
        pieces = ahead_of(slot, fast, early[0])
        slow_more, fast_more = received(pieces, slow, fast), received(pieces, fast, fast)
        pieces = near_of(slot, slow)
        for half, value in ((slow, slow_part), (fast, fast_part)):
            value = divided(value + received(pieces, half, slow), half)
            middle[half] = value
            note(value, half)
        pieces = pieces_of(jnp.concatenate([middle[0], middle[1]], axis=1))
        slow_part = slow_more + own_product(pieces, slow, 2 * slot + 1)
        fast_part = fast_more + own_product(pieces, fast, 2 * slot + 1)
        return slow_part, fast_part, ahead_of(slot, slow, early[1])

    def step(slot, carry):
        advance(slot + 1, *couple(slot), 2 * slot + 2, True)
        return carry

    lax.fori_loop(1, PAIRS, step, 0)
    slow_part, fast_part, pieces = couple(PAIRS)
    for half, value in ((slow, slow_part), (fast, fast_part)):
        total[half] += divided(value + received(pieces, half, slow), half)

    places = []
    for block in range(8):
        place = jnp.int32(0)
        for i in range(1, 8):
            place = place + jnp.where(ids[i] == block, i, 0)
        places.append(place)
    summed = product(backward[...], reorder(jnp.concatenate([total[0], total[1]], axis=1), places))
    early, late = summed[:HALF], summed[HALF:]
    ysend[...] = jnp.where(first, late, early)
    ycopy = remote(ysend, yrecv, last_sems.at[0], last_sems.at[1], (other, shard))
    ycopy.start()

    first_own.wait_send()
    for side in range(2):

        @pl.when(has(side))
        def _():
            for case in range(2):
                first_halo(side, case, group).wait_send()
            matrix_rows(side).wait_send()
            row_facts(side).wait_send()
            passed_on(side).wait_send()
            for slot in range(PAIRS + 1):
                field_near(slot, side).wait_send()
            for slot in range(1, PAIRS + 1):
                part_near(slot, side).wait_send()

        @pl.when(has_far(side))
        def _():
            for slot in range(1, PAIRS + 1):
                field_far(slot, side).wait_send()

    kept = jnp.where(first, early, late)
    ycopy.wait()
    came = yrecv[...]
    out[:, 0, :] = jnp.where(first, kept, came)
    out[:, 1, :] = jnp.where(first, came, kept)


def per_device(adj_source, terminal, capacity, blocks, columns, face_lists):
    nodes = capacity.shape[0]
    half = nodes // 2
    forward, backward, coefs = tables()
    hbm = pl.BlockSpec(memory_space=pltpu.HBM)
    f32, bf16, i32 = jnp.float32, jnp.bfloat16, jnp.int32
    dma = pltpu.SemaphoreType.DMA
    return pl.pallas_call(
        kernel,
        out_shape=pltpu.VMEM(adj_source.shape, f32),
        in_specs=[hbm] * 9,
        out_specs=pl.BlockSpec(memory_space=pltpu.VMEM),
        scratch_shapes=[
            pltpu.VMEM(adj_source.shape, f32),
            pltpu.VMEM(terminal.shape, f32),
            pltpu.VMEM((1, nodes), f32),
            pltpu.SMEM(columns.shape, i32),
            pltpu.SMEM(face_lists.shape, i32),
            pltpu.VMEM(forward.shape, bf16),
            pltpu.VMEM(backward.shape, bf16),
            pltpu.VMEM(coefs.shape, f32),
            pltpu.VMEM(blocks.shape, f32),
            pltpu.VMEM((4, 7, BLOCK, LANES), f32),
            pltpu.VMEM((32, LANES), i32),
            pltpu.VMEM((2, 16 * BLOCK, half), bf16),
            pltpu.VMEM((2, 16 * BLOCK, half), bf16),
            pltpu.VMEM((2, 8 * BLOCK, half), bf16),
            pltpu.VMEM((2, 8 * BLOCK, half), bf16),
            pltpu.VMEM((2, 8, half), f32),
            pltpu.VMEM((2, 3, HALF, half), f32),
            pltpu.VMEM((2, 3, HALF, half), f32),
            pltpu.VMEM((2, 8, half), f32),
            pltpu.VMEM((2, 32, LANES), f32),
            pltpu.VMEM((2, 32, LANES), f32),
            pltpu.VMEM((2, 2, 6, BLOCK, LANES), f32),
            pltpu.VMEM((2, 2, STEPS, half), f32),
            pltpu.VMEM((2, 2, STEPS, half), f32),
            pltpu.VMEM((2, STEPS, half), f32),
            pltpu.VMEM((PAIRS + 1, 2, STEPS, half), f32),
            pltpu.VMEM((PAIRS + 1, 2, STEPS, half), f32),
            pltpu.VMEM((PAIRS + 1, 2, STEPS, half), f32),
            pltpu.VMEM((PAIRS + 1, 2, STEPS, half), f32),
            pltpu.VMEM((PAIRS + 1, 2, STEPS, half), f32),
            pltpu.VMEM((PAIRS + 1, 2, STEPS, half), f32),
            pltpu.VMEM((2, STEPS, half), f32),
            pltpu.VMEM((2, 8, half), f32),
            pltpu.VMEM((2, STEPS, half), f32),
            pltpu.VMEM((HALF, nodes), f32),
            pltpu.VMEM((HALF, nodes), f32),
            dma((9,)),
            dma((5,)),
            dma((5,)),
            dma((6,)),
            dma((6,)),
            dma((2,)),
            dma((PAIRS + 1, 3, 2)),
            dma((PAIRS + 1, 3, 2)),
        ],
        compiler_params=pltpu.CompilerParams(
            collective_id=0, has_side_effects=True, vmem_limit_bytes=60 * 1024 * 1024
        ),
        name="window",
    )(
        adj_source, terminal, capacity.reshape(1, nodes), columns, face_lists,
        jnp.asarray(forward), jnp.asarray(backward), jnp.asarray(coefs), blocks,
    )


def solution(mesh):
    return jax.shard_map(
        per_device,
        mesh=mesh,
        in_specs=(
            P("tm", None, "space"),
            P(None, "space"),
            P("space"),
            P("space", None, None, None),
            P("space", None),
            P("space", None, None),
        ),
        out_specs=P("tm", None, "space"),
        check_vma=False,
    )
```

```python
import functools
import math

import jax
import jax.numpy as jnp
import numpy as np
from jax import lax
from jax.experimental import pallas as pl
from jax.experimental.pallas import tpu as pltpu
from jax.sharding import PartitionSpec as P

OUTER = 3
SWEEPS = 3
STEPS = 32
HALF = STEPS // 2
CORNER_WEIGHT = 0.1
ROOT = CORNER_WEIGHT ** (1.0 / STEPS)
PAIRS = (OUTER * SWEEPS - 3) // 2
BLOCK = 64
LANES = 128
MESH = pl.DeviceIdType.MESH


def split(value):
    high = value.astype(jnp.bfloat16)
    low = (value - high.astype(jnp.float32)).astype(jnp.bfloat16)
    return high, low


def split_table(table):
    high = table.astype(jnp.bfloat16)
    low = (table - high.astype(np.float64)).astype(jnp.bfloat16)
    return np.concatenate([high, high, low], axis=1)


def tables():
    steps = np.arange(STEPS)
    modes = np.arange(HALF)
    angles = 2.0 * np.pi * ((modes[:, None] * steps[None, :]) % STEPS) / STEPS
    nyquist = (-1.0) ** steps
    cosines, sines = np.cos(angles), -np.sin(angles)
    sines[0] = nyquist
    basis = np.concatenate([cosines, sines], axis=0)
    scale = CORNER_WEIGHT ** (steps / STEPS)
    forward = basis * scale[None, :]
    weight = np.full((STEPS,), 2.0)
    weight[0] = weight[HALF] = 1.0
    inverse = (basis * weight[:, None]).T / STEPS
    last = inverse[STEPS - 1] * ROOT
    backward = inverse / scale[:, None]
    real_coef = 1.0 - ROOT * np.cos(2.0 * np.pi * modes / STEPS)
    imag_coef = ROOT * np.sin(2.0 * np.pi * modes / STEPS)
    real_low = real_coef.copy()
    real_low[0] = 1.0 + ROOT
    columns = np.zeros((STEPS, LANES), np.float32)
    columns[:HALF, 0] = real_coef
    columns[HALF:, 0] = real_low
    columns[:HALF, 1] = imag_coef
    columns[:, 2] = last
    halves = [split_table(forward[:, part * HALF : (part + 1) * HALF]) for part in range(2)]
    return np.stack(halves), split_table(backward), columns


def product(table, value):
    high, low = split(value)
    return jnp.dot(
        table, jnp.concatenate([high, low, high], axis=0), preferred_element_type=jnp.float32
    )


def reorder(value, ids):
    lower_half = lax.broadcasted_iota(jnp.int32, (1, LANES), 1) < BLOCK
    both = []
    for tile in range(4):
        plain = value[:, tile * LANES : (tile + 1) * LANES]
        turned = pltpu.roll(plain, BLOCK, 1)
        both.append(jnp.where(lower_half, plain, turned))
        both.append(jnp.where(lower_half, turned, plain))
    tiles = []
    for tile in range(4):
        wanted = jnp.where(lower_half, ids[2 * tile], ids[2 * tile + 1])
        total = both[0]
        for block in range(1, 8):
            total = jnp.where(wanted == block, both[block], total)
        tiles.append(total)
    return jnp.concatenate(tiles, axis=1)


def kernel(
    adj_hbm, term_hbm, cap_hbm, cols_hbm, faces_hbm, forward_hbm, backward_hbm, coefs_hbm,
    blocks_hbm, out,
    adj, term, cap, cols, faces, forward, backward, coefs, own_blk, blk,
    turned, names, mat_high, mat_low, face_high, face_low, diag, recip, face_recip, capacity,
    meta, met, tiles, psend, precv, pown, wsend, near, far, own_part, part_send, part, middle, tails, total, ysend, yrecv,
    load_sems, first_send, first_recv, once_send, once_recv, last_sems, send_sems, recv_sems,
):
    group = lax.axis_index("tm")
    shard = lax.axis_index("space")
    shards = lax.axis_size("space")
    other = 1 - group
    first = group == 0
    slow = jnp.where(lax.rem(shard, 4) >= 2, 1, 0)
    fast = 1 - slow
    order = (fast, slow)

    def has(side):
        return jnp.where(side == 0, shard > 0, shard < shards - 1)

    def has_far(side):
        return jnp.where(side == 0, shard > 1, shard < shards - 2)

    def beside(side):
        return jnp.clip(shard + 2 * side - 1, 0, shards - 1)

    def beyond(side):
        return jnp.clip(shard + 4 * side - 2, 0, shards - 1)

    barrier = pltpu.get_barrier_semaphore()

    def greet(target):
        pl.semaphore_signal(barrier, inc=1, device_id=target, device_id_type=MESH)

    greets = 1
    for side in range(2):

        @pl.when(has(side))
        def _():
            greet((0, beside(side)))
            greet((1, beside(side)))

        greets = greets + 2 * has(side).astype(jnp.int32)

    greet((other, shard))

    loads = [
        pltpu.make_async_copy(source, target, load_sems.at[i])
        for i, (source, target) in enumerate(
            [
                (faces_hbm, faces), (blocks_hbm.at[:, 0], own_blk),
                (coefs_hbm, coefs), (cap_hbm, cap), (adj_hbm, adj), (term_hbm, term),
                (forward_hbm, forward), (cols_hbm, cols),
                (blocks_hbm.at[:, pl.ds(1, 6)], blk), (backward_hbm, backward),
            ]
        )
    ]
    for load in loads:
        load.start()

    for side in range(2):

        @pl.when(jnp.logical_not(has_far(side)))
        def _():
            far[:, side] = jnp.zeros_like(far[:, side])

        @pl.when(jnp.logical_not(has(side)))
        def _():
            near[:, side] = jnp.zeros_like(near[:, side])
            part[:, side] = jnp.zeros_like(part[:, side])
            precv[:, side] = jnp.zeros_like(precv[:, side])
            tiles[side] = jnp.zeros_like(tiles[side])
            met[side] = jnp.ones_like(met[side])

    for load in loads[:7]:
        load.wait()

    ids = [faces[0, i // 4, i % 4] for i in range(8)]
    cap_row = cap[...]
    cap_own = reorder(jnp.broadcast_to(cap_row, (8, 8 * BLOCK)), ids)
    eye = lax.broadcasted_iota(jnp.int32, (BLOCK, BLOCK), 0) == lax.broadcasted_iota(
        jnp.int32, (BLOCK, BLOCK), 1
    )
    rows = [
        jnp.sum(jnp.where(eye, own_blk[ids[i]], 0.0), axis=0, keepdims=True) for i in range(8)
    ]
    diag_own = jnp.broadcast_to(jnp.concatenate(rows, axis=1), (8, 8 * BLOCK))
    for half in range(2):
        capacity[half] = cap_own[:, half * 4 * BLOCK : (half + 1) * 4 * BLOCK]
        diag[half] = diag_own[:, half * 4 * BLOCK : (half + 1) * 4 * BLOCK]

    def reciprocals(cap_part, diag_part):
        imag = coefs[0:HALF, 1:2] * cap_part
        found = []
        for half in range(2):
            real = coefs[half * HALF : (half + 1) * HALF, 0:1] * cap_part + diag_part
            over = 1.0 / (real * real + imag * imag)
            found.append(real * over)
            if half == 0:
                turn = -imag * over
        return found[0], found[1], turn

    def divide(value, upper_real, lower_real, turn):
        upper_part, lower_part = value[:HALF], value[HALF:]
        return jnp.concatenate(
            [
                upper_real * upper_part - turn * lower_part,
                turn * upper_part + lower_real * lower_part,
            ],
            axis=0,
        )

    for half in range(2):
        recip[half, 0], recip[half, 1], recip[half, 2] = reciprocals(
            capacity[half, 0:1], diag[half, 0:1]
        )

    def divided(value, half):
        return divide(value, recip[half, 0], recip[half, 1], recip[half, 2])

    head_row = first & (lax.broadcasted_iota(jnp.int32, (HALF, 1), 0) == 0)
    for case in range(2):
        source = adj[:, case, :] + jnp.where(head_row, term[case : case + 1, :] * cap_row, 0.0)
        spectrum = reorder(product(forward[group], source), ids)
        psend[case, 0] = divided(spectrum[:, : 4 * BLOCK], 0)
        psend[case, 1] = divided(spectrum[:, 4 * BLOCK :], 1)

    pl.semaphore_wait(barrier, greets)

    def remote(source, target, send_sem, recv_sem, device):
        return pltpu.make_async_remote_copy(
            src_ref=source, dst_ref=target, send_sem=send_sem, recv_sem=recv_sem,
            device_id=device, device_id_type=MESH,
        )

    def first_halo(side, case, sender):
        return remote(
            psend.at[case, side], precv.at[sender, 1 - side],
            first_send.at[2 * side + case], first_recv.at[2 * (1 - side) + sender],
            (case, beside(side)),
        )

    first_own = remote(
        psend.at[other], pown, first_send.at[4], first_recv.at[4], (other, shard)
    )

    def matrix_rows(side):
        return remote(
            turned.at[2 * side + group, pl.ds(1, 6)], tiles.at[1 - side, group],
            once_send.at[side], once_recv.at[1 - side], (group, beside(side)),
        )

    def row_facts(side):
        return remote(
            meta.at[side], met.at[1 - side],
            once_send.at[2 + side], once_recv.at[3 - side], (group, beside(side)),
        )

    def passed_on(side):
        return remote(
            tiles.at[side, group], tiles.at[side, group],
            once_send.at[4 + side], once_recv.at[4 + side], (other, shard),
        )

    def field_near(slot, side):
        return remote(
            wsend.at[slot, side], near.at[slot, 1 - side],
            send_sems.at[slot, 0, side], recv_sems.at[slot, 0, 1 - side], (group, beside(side)),
        )

    def field_far(slot, side):
        return remote(
            wsend.at[slot, side], far.at[slot, 1 - side],
            send_sems.at[slot, 1, side], recv_sems.at[slot, 1, 1 - side], (group, beyond(side)),
        )

    def part_near(slot, side):
        return remote(
            part_send.at[slot, side], part.at[slot, 1 - side],
            send_sems.at[slot, 2, side], recv_sems.at[slot, 2, 1 - side], (group, beside(side)),
        )

    for side in (slow, fast):

        @pl.when(has(side))
        def _():
            for case in range(2):
                first_halo(side, case, group).start()

    first_own.start()
    for load in loads[7:]:
        load.wait()

    lower_half = lax.broadcasted_iota(jnp.int32, (1, LANES), 1) < BLOCK
    turned_eye = lax.broadcasted_iota(jnp.int32, (BLOCK, LANES), 0) == lax.rem(
        lax.broadcasted_iota(jnp.int32, (BLOCK, LANES), 1), BLOCK
    )
    for pair in range(4):
        left, right = ids[2 * pair], ids[2 * pair + 1]
        for k in range(7):
            both = [blk[at, k - 1] if k else own_blk[at] for at in (left, right)]
            entry = jnp.concatenate(both, axis=0)
            entry = -entry.T
            if k == 0:
                entry = jnp.where(turned_eye, 0.0, entry)
            turned[pair, k] = entry
            names[8 * pair + k : 8 * pair + k + 1, :] = jnp.where(
                lower_half, cols[left, k], cols[right, k]
            )
        names[8 * pair + 7 : 8 * pair + 8, :] = jnp.full((1, LANES), -1, jnp.int32)
    raw = names[...]
    place_of = jnp.zeros_like(raw)
    for i in range(8):
        place_of = jnp.where(raw == ids[i], i, place_of)
    place_of = jnp.where(raw >= 8, jnp.where(has(0), raw, -1), place_of)
    place_of = jnp.where(raw >= 12, jnp.where(has(1), raw, -1), place_of)
    named = place_of.astype(jnp.float32)
    for side in range(2):
        meta[side, 0:16] = named[16 * side : 16 * side + 16]
        for row, table in ((16, capacity), (24, diag)):
            for pair in range(2):
                meta[side, row + 4 * pair : row + 4 * pair + 4] = table[
                    side, 0:4, pair * LANES : (pair + 1) * LANES
                ]
    for side in range(2):

        @pl.when(has(side))
        def _():
            row_facts(side).start()
            matrix_rows(side).start()

    for pair in range(4):
        wanted = [named[8 * pair + k : 8 * pair + k + 1] for k in range(7)]

        def build(place, carry, pair=pair, wanted=wanted):
            name = place.astype(jnp.float32)
            tile = jnp.where(wanted[0] == name, turned[pair, 0], 0.0)
            for k in range(1, 7):
                tile = tile + jnp.where(wanted[k] == name, turned[pair, k], 0.0)
            high, low = split(tile)
            at = pl.ds(pl.multiple_of(place * BLOCK, BLOCK), BLOCK)
            lanes = slice(pair % 2 * LANES, (pair % 2 + 1) * LANES)
            mat_high[pair // 2, at, lanes] = high
            mat_low[pair // 2, at, lanes] = low
            return carry

        lax.fori_loop(0, 16, build, 0)

    def pieces_of(value):
        high, low = split(value)
        return high, jnp.concatenate([high, low], axis=0)

    def times(pieces, matrix_high, matrix_low):
        high, stacked = pieces
        both = jnp.dot(stacked, matrix_high, preferred_element_type=jnp.float32)
        rest = jnp.dot(high, matrix_low, preferred_element_type=jnp.float32)
        return both[:STEPS] + both[STEPS:] + rest

    def rows_of(side):
        return pl.ds(pl.multiple_of(side * (4 * BLOCK), 4 * BLOCK), 4 * BLOCK)

    def received(pieces, half, side):
        rows = rows_of(2 + side)
        return times(pieces, mat_high[half, rows, :], mat_low[half, rows, :])

    def face(value, side, from_side):
        rows = rows_of(from_side)
        return times(pieces_of(value), face_high[side, rows, :], face_low[side, rows, :])

    real_rows = lax.broadcasted_iota(jnp.int32, (STEPS, 1), 0) <= HALF
    last = coefs[:, 2:3]

    def note(value, half):
        total[half] += value
        weighted = value * last
        tails[half] += weighted[0:8] + weighted[8:16] + weighted[16:24] + weighted[24:32]

    def own_product(pieces, half, application):
        closes = lax.rem(application, SWEEPS) == SWEEPS - 1
        tail = jnp.sum(tails[half], axis=0, keepdims=True)
        fix = jnp.where(closes, tail, 0.0) * capacity[half, 0:1]
        tails[half] = jnp.where(closes, 0.0, tails[half])
        result = times(
            pieces, mat_high[half, 0 : 8 * BLOCK, :], mat_low[half, 0 : 8 * BLOCK, :]
        )
        return result - jnp.where(real_rows, fix, 0.0)

    def send_field(slot, side, paired):
        @pl.when(has(side))
        def _():
            field_near(slot, side).start()

        if paired:

            @pl.when(has_far(side))
            def _():
                field_far(slot, side).start()

    def advance(slot, slow_part, fast_part, pieces, application, paired):
        for half, value in ((slow, slow_part), (fast, fast_part)):
            value = divided(value + received(pieces, half, slow), half)
            wsend[slot, half] = value
            send_field(slot, half, paired)
            note(value, half)
        pieces = pieces_of(jnp.concatenate([wsend[slot, 0], wsend[slot, 1]], axis=1))
        for half in (slow, fast):
            result = own_product(pieces, half, application)
            own_part[slot, half] = result
            if paired:
                part_send[slot, half] = divided(result, half)

                @pl.when(has(half))
                def _():
                    part_near(slot, half).start()

    def near_of(slot, side):
        @pl.when(has(side))
        def _():
            field_near(slot, 1 - side).wait_recv()

        return pieces_of(near[slot, side])

    def add_fast(slow_part, fast_part, pieces):
        return slow_part + received(pieces, slow, fast), fast_part + received(pieces, fast, fast)

    def begun(slot):
        return add_fast(own_part[slot, slow], own_part[slot, fast], near_of(slot, fast))

    total[...] = jnp.zeros_like(total)
    tails[...] = jnp.zeros_like(tails)
    first_own.wait_recv()
    halves = [psend[group, half] + pown[half] for half in range(2)]
    for half in range(2):
        note(halves[half], half)
    pieces = pieces_of(jnp.concatenate(halves, axis=1))
    slow_part = own_product(pieces, slow, jnp.int32(0))
    fast_part = own_product(pieces, fast, jnp.int32(0))
    for side in order:

        @pl.when(has(side))
        def _():
            for sender in range(2):
                first_halo(1 - side, 0, sender).wait_recv()

        pieces = pieces_of(precv[0, side] + precv[1, side])
        if side is fast:
            slow_part, fast_part = add_fast(slow_part, fast_part, pieces)
    advance(0, slow_part, fast_part, pieces, jnp.int32(1), False)

    advance(1, *begun(0), near_of(0, slow), jnp.int32(2), True)

    for side in range(2):

        @pl.when(has(side))
        def _():
            matrix_rows(1 - side).wait_recv()
            passed_on(side).start()

    for side in range(2):

        @pl.when(has(side))
        def _():
            row_facts(1 - side).wait_recv()

        face_recip[side, 0], face_recip[side, 1], face_recip[side, 2] = reciprocals(
            jnp.concatenate([met[side, 16:17], met[side, 20:21]], axis=1),
            jnp.concatenate([met[side, 24:25], met[side, 28:29]], axis=1),
        )

        @pl.when(has(side))
        def _():
            passed_on(side).wait_recv()

        for pair in range(2):

            def build(place, carry, side=side, pair=pair):
                name = (place + 8).astype(jnp.float32)
                tile = jnp.where(
                    met[side, 8 * pair + 1 : 8 * pair + 2] == name, tiles[side, pair, 0], 0.0
                )
                for k in range(2, 7):
                    wanted = met[side, 8 * pair + k : 8 * pair + k + 1]
                    tile = tile + jnp.where(wanted == name, tiles[side, pair, k - 1], 0.0)
                high, low = split(tile)
                at = pl.ds(pl.multiple_of(place * BLOCK, BLOCK), BLOCK)
                face_high[side, at, pair * LANES : (pair + 1) * LANES] = high
                face_low[side, at, pair * LANES : (pair + 1) * LANES] = low
                return carry

            lax.fori_loop(0, 8, build, 0)

    def ahead_of(slot, side, early):
        @pl.when(has_far(side))
        def _():
            field_far(slot, 1 - side).wait_recv()

        found = divide(
            early + face(far[slot, side], side, side),
            face_recip[side, 0], face_recip[side, 1], face_recip[side, 2],
        )

        @pl.when(has(side))
        def _():
            part_near(slot, 1 - side).wait_recv()

        return pieces_of(found + part[slot, side])

    def couple(slot):
        early = [face(wsend[slot, side], side, 1 - side) for side in order]
        slow_part, fast_part = begun(slot)
        pieces = ahead_of(slot, fast, early[0])
        slow_more, fast_more = received(pieces, slow, fast), received(pieces, fast, fast)
        pieces = near_of(slot, slow)
        for half, value in ((slow, slow_part), (fast, fast_part)):
            value = divided(value + received(pieces, half, slow), half)
            middle[half] = value
            note(value, half)
        pieces = pieces_of(jnp.concatenate([middle[0], middle[1]], axis=1))
        slow_part = slow_more + own_product(pieces, slow, 2 * slot + 1)
        fast_part = fast_more + own_product(pieces, fast, 2 * slot + 1)
        return slow_part, fast_part, ahead_of(slot, slow, early[1])

    def step(slot, carry):
        advance(slot + 1, *couple(slot), 2 * slot + 2, True)
        return carry

    lax.fori_loop(1, PAIRS, step, 0)
    slow_part, fast_part, pieces = couple(PAIRS)
    for half, value in ((slow, slow_part), (fast, fast_part)):
        total[half] += divided(value + received(pieces, half, slow), half)

    places = []
    for block in range(8):
        place = jnp.int32(0)
        for i in range(1, 8):
            place = place + jnp.where(ids[i] == block, i, 0)
        places.append(place)
    summed = product(backward[...], reorder(jnp.concatenate([total[0], total[1]], axis=1), places))
    early, late = summed[:HALF], summed[HALF:]
    ysend[...] = jnp.where(first, late, early)
    ycopy = remote(ysend, yrecv, last_sems.at[0], last_sems.at[1], (other, shard))
    ycopy.start()

    first_own.wait_send()
    for side in range(2):

        @pl.when(has(side))
        def _():
            for case in range(2):
                first_halo(side, case, group).wait_send()
            matrix_rows(side).wait_send()
            row_facts(side).wait_send()
            passed_on(side).wait_send()
            for slot in range(PAIRS + 1):
                field_near(slot, side).wait_send()
            for slot in range(1, PAIRS + 1):
                part_near(slot, side).wait_send()

        @pl.when(has_far(side))
        def _():
            for slot in range(1, PAIRS + 1):
                field_far(slot, side).wait_send()

    kept = jnp.where(first, early, late)
    ycopy.wait()
    came = yrecv[...]
    out[:, 0, :] = jnp.where(first, kept, came)
    out[:, 1, :] = jnp.where(first, came, kept)


def per_device(adj_source, terminal, capacity, blocks, columns, face_lists):
    nodes = capacity.shape[0]
    half = nodes // 2
    forward, backward, coefs = tables()
    hbm = pl.BlockSpec(memory_space=pltpu.HBM)
    f32, bf16, i32 = jnp.float32, jnp.bfloat16, jnp.int32
    dma = pltpu.SemaphoreType.DMA
    return pl.pallas_call(
        kernel,
        out_shape=pltpu.VMEM(adj_source.shape, f32),
        in_specs=[hbm] * 9,
        out_specs=pl.BlockSpec(memory_space=pltpu.VMEM),
        scratch_shapes=[
            pltpu.VMEM(adj_source.shape, f32),
            pltpu.VMEM(terminal.shape, f32),
            pltpu.VMEM((1, nodes), f32),
            pltpu.SMEM(columns.shape, i32),
            pltpu.SMEM(face_lists.shape, i32),
            pltpu.VMEM(forward.shape, bf16),
            pltpu.VMEM(backward.shape, bf16),
            pltpu.VMEM(coefs.shape, f32),
            pltpu.VMEM((8, BLOCK, BLOCK), f32),
            pltpu.VMEM((8, 6, BLOCK, BLOCK), f32),
            pltpu.VMEM((4, 7, BLOCK, LANES), f32),
            pltpu.VMEM((32, LANES), i32),
            pltpu.VMEM((2, 16 * BLOCK, half), bf16),
            pltpu.VMEM((2, 16 * BLOCK, half), bf16),
            pltpu.VMEM((2, 8 * BLOCK, half), bf16),
            pltpu.VMEM((2, 8 * BLOCK, half), bf16),
            pltpu.VMEM((2, 8, half), f32),
            pltpu.VMEM((2, 3, HALF, half), f32),
            pltpu.VMEM((2, 3, HALF, half), f32),
            pltpu.VMEM((2, 8, half), f32),
            pltpu.VMEM((2, 32, LANES), f32),
            pltpu.VMEM((2, 32, LANES), f32),
            pltpu.VMEM((2, 2, 6, BLOCK, LANES), f32),
            pltpu.VMEM((2, 2, STEPS, half), f32),
            pltpu.VMEM((2, 2, STEPS, half), f32),
            pltpu.VMEM((2, STEPS, half), f32),
            pltpu.VMEM((PAIRS + 1, 2, STEPS, half), f32),
            pltpu.VMEM((PAIRS + 1, 2, STEPS, half), f32),
            pltpu.VMEM((PAIRS + 1, 2, STEPS, half), f32),
            pltpu.VMEM((PAIRS + 1, 2, STEPS, half), f32),
            pltpu.VMEM((PAIRS + 1, 2, STEPS, half), f32),
            pltpu.VMEM((PAIRS + 1, 2, STEPS, half), f32),
            pltpu.VMEM((2, STEPS, half), f32),
            pltpu.VMEM((2, 8, half), f32),
            pltpu.VMEM((2, STEPS, half), f32),
            pltpu.VMEM((HALF, nodes), f32),
            pltpu.VMEM((HALF, nodes), f32),
            dma((10,)),
            dma((5,)),
            dma((5,)),
            dma((6,)),
            dma((6,)),
            dma((2,)),
            dma((PAIRS + 1, 3, 2)),
            dma((PAIRS + 1, 3, 2)),
        ],
        compiler_params=pltpu.CompilerParams(
            collective_id=0, has_side_effects=True, vmem_limit_bytes=60 * 1024 * 1024
        ),
        name="window",
    )(
        adj_source, terminal, capacity.reshape(1, nodes), columns, face_lists,
        jnp.asarray(forward), jnp.asarray(backward), jnp.asarray(coefs), blocks,
    )


def solution(mesh):
    return jax.shard_map(
        per_device,
        mesh=mesh,
        in_specs=(
            P("tm", None, "space"),
            P(None, "space"),
            P("space"),
            P("space", None, None, None),
            P("space", None),
            P("space", None, None),
        ),
        out_specs=P("tm", None, "space"),
        check_vma=False,
    )
```

```python
import functools
import math

import jax
import jax.numpy as jnp
import numpy as np
from jax import lax
from jax.experimental import pallas as pl
from jax.experimental.pallas import tpu as pltpu
from jax.sharding import PartitionSpec as P

OUTER = 3
SWEEPS = 3
STEPS = 32
HALF = STEPS // 2
CORNER_WEIGHT = 0.1
ROOT = CORNER_WEIGHT ** (1.0 / STEPS)
PAIRS = (OUTER * SWEEPS - 3) // 2
BLOCK = 64
LANES = 128
MESH = pl.DeviceIdType.MESH


def split(value):
    high = value.astype(jnp.bfloat16)
    low = (value - high.astype(jnp.float32)).astype(jnp.bfloat16)
    return high, low


def split_table(table):
    high = table.astype(jnp.bfloat16)
    low = (table - high.astype(np.float64)).astype(jnp.bfloat16)
    return np.concatenate([high, high, low], axis=1)


def tables():
    steps = np.arange(STEPS)
    modes = np.arange(HALF)
    angles = 2.0 * np.pi * ((modes[:, None] * steps[None, :]) % STEPS) / STEPS
    nyquist = (-1.0) ** steps
    cosines, sines = np.cos(angles), -np.sin(angles)
    sines[0] = nyquist
    basis = np.concatenate([cosines, sines], axis=0)
    scale = CORNER_WEIGHT ** (steps / STEPS)
    forward = basis * scale[None, :]
    weight = np.full((STEPS,), 2.0)
    weight[0] = weight[HALF] = 1.0
    inverse = (basis * weight[:, None]).T / STEPS
    last = inverse[STEPS - 1] * ROOT
    backward = inverse / scale[:, None]
    real_coef = 1.0 - ROOT * np.cos(2.0 * np.pi * modes / STEPS)
    imag_coef = ROOT * np.sin(2.0 * np.pi * modes / STEPS)
    real_low = real_coef.copy()
    real_low[0] = 1.0 + ROOT
    columns = np.zeros((STEPS, LANES), np.float32)
    columns[:HALF, 0] = real_coef
    columns[HALF:, 0] = real_low
    columns[:HALF, 1] = imag_coef
    columns[:, 2] = last
    halves = [split_table(forward[:, part * HALF : (part + 1) * HALF]) for part in range(2)]
    return np.stack(halves), split_table(backward), columns


def product(table, value):
    high, low = split(value)
    return jnp.dot(
        table, jnp.concatenate([high, low, high], axis=0), preferred_element_type=jnp.float32
    )


def reorder(value, ids):
    lower_half = lax.broadcasted_iota(jnp.int32, (1, LANES), 1) < BLOCK
    both = []
    for tile in range(4):
        plain = value[:, tile * LANES : (tile + 1) * LANES]
        turned = pltpu.roll(plain, BLOCK, 1)
        both.append(jnp.where(lower_half, plain, turned))
        both.append(jnp.where(lower_half, turned, plain))
    tiles = []
    for tile in range(4):
        wanted = jnp.where(lower_half, ids[2 * tile], ids[2 * tile + 1])
        total = both[0]
        for block in range(1, 8):
            total = jnp.where(wanted == block, both[block], total)
        tiles.append(total)
    return jnp.concatenate(tiles, axis=1)


def kernel(
    adj_hbm, term_hbm, cap_hbm, cols_hbm, faces_hbm, forward_hbm, backward_hbm, coefs_hbm,
    blocks_hbm, out,
    adj, term, cap, cols, faces, forward, backward, coefs, own_blk, blk,
    turned, names, mat_high, mat_low, face_high, face_low, diag, recip, face_recip, capacity,
    meta, met, tiles, psend, precv, pown, wsend, near, far, own_part, part_send, part, middle, tails, total, ysend, yrecv,
    load_sems, first_send, first_recv, once_send, once_recv, last_sems, send_sems, recv_sems,
):
    group = lax.axis_index("tm")
    shard = lax.axis_index("space")
    shards = lax.axis_size("space")
    other = 1 - group
    first = group == 0
    slow = jnp.where(lax.rem(shard, 4) >= 2, 1, 0)
    fast = 1 - slow
    order = (fast, slow)

    def has(side):
        return jnp.where(side == 0, shard > 0, shard < shards - 1)

    def has_far(side):
        return jnp.where(side == 0, shard > 1, shard < shards - 2)

    def beside(side):
        return jnp.clip(shard + 2 * side - 1, 0, shards - 1)

    def beyond(side):
        return jnp.clip(shard + 4 * side - 2, 0, shards - 1)

    barrier = pltpu.get_barrier_semaphore()

    def greet(target):
        pl.semaphore_signal(barrier, inc=1, device_id=target, device_id_type=MESH)

    greets = 1
    for side in range(2):

        @pl.when(has(side))
        def _():
            greet((0, beside(side)))
            greet((1, beside(side)))

        greets = greets + 2 * has(side).astype(jnp.int32)

    greet((other, shard))

    loads = [
        pltpu.make_async_copy(source, target, load_sems.at[i])
        for i, (source, target) in enumerate(
            [
                (faces_hbm, faces), (blocks_hbm.at[:, 0], own_blk),
                (coefs_hbm, coefs), (cap_hbm, cap), (adj_hbm, adj), (term_hbm, term),
                (forward_hbm, forward), (cols_hbm, cols),
                (blocks_hbm.at[:, pl.ds(1, 6)], blk), (backward_hbm, backward),
            ]
        )
    ]
    for load in loads:
        load.start()

    for side in range(2):

        @pl.when(jnp.logical_not(has_far(side)))
        def _():
            far[:, side] = jnp.zeros_like(far[:, side])

        @pl.when(jnp.logical_not(has(side)))
        def _():
            near[:, side] = jnp.zeros_like(near[:, side])
            part[:, side] = jnp.zeros_like(part[:, side])
            precv[:, side] = jnp.zeros_like(precv[:, side])
            tiles[side] = jnp.zeros_like(tiles[side])
            met[side] = jnp.ones_like(met[side])

    for load in loads[:7]:
        load.wait()

    ids = [faces[0, i // 4, i % 4] for i in range(8)]
    cap_row = cap[...]
    cap_own = reorder(jnp.broadcast_to(cap_row, (8, 8 * BLOCK)), ids)
    eye = lax.broadcasted_iota(jnp.int32, (BLOCK, BLOCK), 0) == lax.broadcasted_iota(
        jnp.int32, (BLOCK, BLOCK), 1
    )
    rows = [
        jnp.sum(jnp.where(eye, own_blk[ids[i]], 0.0), axis=0, keepdims=True) for i in range(8)
    ]
    diag_own = jnp.broadcast_to(jnp.concatenate(rows, axis=1), (8, 8 * BLOCK))
    for half in range(2):
        capacity[half] = cap_own[:, half * 4 * BLOCK : (half + 1) * 4 * BLOCK]
        diag[half] = diag_own[:, half * 4 * BLOCK : (half + 1) * 4 * BLOCK]

    def reciprocals(cap_part, diag_part):
        imag = coefs[0:HALF, 1:2] * cap_part
        found = []
        for half in range(2):
            real = coefs[half * HALF : (half + 1) * HALF, 0:1] * cap_part + diag_part
            over = 1.0 / (real * real + imag * imag)
            found.append(real * over)
            if half == 0:
                turn = -imag * over
        return found[0], found[1], turn

    def divide(value, upper_real, lower_real, turn):
        upper_part, lower_part = value[:HALF], value[HALF:]
        return jnp.concatenate(
            [
                upper_real * upper_part - turn * lower_part,
                turn * upper_part + lower_real * lower_part,
            ],
            axis=0,
        )

    for half in range(2):
        recip[half, 0], recip[half, 1], recip[half, 2] = reciprocals(
            capacity[half, 0:1], diag[half, 0:1]
        )

    def divided(value, half):
        return divide(value, recip[half, 0], recip[half, 1], recip[half, 2])

    head_row = first & (lax.broadcasted_iota(jnp.int32, (HALF, 1), 0) == 0)
    for case in range(2):
        source = adj[:, case, :] + jnp.where(head_row, term[case : case + 1, :] * cap_row, 0.0)
        spectrum = reorder(product(forward[group], source), ids)
        psend[case, 0] = divided(spectrum[:, : 4 * BLOCK], 0)
        psend[case, 1] = divided(spectrum[:, 4 * BLOCK :], 1)

    pl.semaphore_wait(barrier, greets)

    def remote(source, target, send_sem, recv_sem, device):
        return pltpu.make_async_remote_copy(
            src_ref=source, dst_ref=target, send_sem=send_sem, recv_sem=recv_sem,
            device_id=device, device_id_type=MESH,
        )

    def first_halo(side, case, sender):
        return remote(
            psend.at[case, side], precv.at[sender, 1 - side],
            first_send.at[2 * side + case], first_recv.at[2 * (1 - side) + sender],
            (case, beside(side)),
        )

    first_own = remote(
        psend.at[other], pown, first_send.at[4], first_recv.at[4], (other, shard)
    )

    def matrix_rows(side):
        return remote(
            turned.at[2 * side + group, pl.ds(1, 6)], tiles.at[1 - side, group],
            once_send.at[side], once_recv.at[1 - side], (group, beside(side)),
        )

    def row_facts(side):
        return remote(
            meta.at[side], met.at[1 - side],
            once_send.at[2 + side], once_recv.at[3 - side], (group, beside(side)),
        )

    def passed_on(side):
        return remote(
            tiles.at[side, group], tiles.at[side, group],
            once_send.at[4 + side], once_recv.at[4 + side], (other, shard),
        )

    def field_near(slot, side):
        return remote(
            wsend.at[slot, side], near.at[slot, 1 - side],
            send_sems.at[slot, 0, side], recv_sems.at[slot, 0, 1 - side], (group, beside(side)),
        )

    def field_far(slot, side):
        return remote(
            wsend.at[slot, side], far.at[slot, 1 - side],
            send_sems.at[slot, 1, side], recv_sems.at[slot, 1, 1 - side], (group, beyond(side)),
        )

    def part_near(slot, side):
        return remote(
            part_send.at[slot, side], part.at[slot, 1 - side],
            send_sems.at[slot, 2, side], recv_sems.at[slot, 2, 1 - side], (group, beside(side)),
        )

    for side in (slow, fast):

        @pl.when(has(side))
        def _():
            for case in range(2):
                first_halo(side, case, group).start()

    first_own.start()
    for load in loads[7:]:
        load.wait()

    lower_half = lax.broadcasted_iota(jnp.int32, (1, LANES), 1) < BLOCK
    turned_eye = lax.broadcasted_iota(jnp.int32, (BLOCK, LANES), 0) == lax.rem(
        lax.broadcasted_iota(jnp.int32, (BLOCK, LANES), 1), BLOCK
    )
    for pair in range(4):
        left, right = ids[2 * pair], ids[2 * pair + 1]
        for k in range(7):
            both = [blk[at, k - 1] if k else own_blk[at] for at in (left, right)]
            entry = jnp.concatenate(both, axis=0)
            entry = -entry.T
            if k == 0:
                entry = jnp.where(turned_eye, 0.0, entry)
            turned[pair, k] = entry
            names[8 * pair + k : 8 * pair + k + 1, :] = jnp.where(
                lower_half, cols[left, k], cols[right, k]
            )
        names[8 * pair + 7 : 8 * pair + 8, :] = jnp.full((1, LANES), -1, jnp.int32)
    raw = names[...]
    place_of = jnp.zeros_like(raw)
    for i in range(8):
        place_of = jnp.where(raw == ids[i], i, place_of)
    place_of = jnp.where(raw >= 8, jnp.where(has(0), raw, -1), place_of)
    place_of = jnp.where(raw >= 12, jnp.where(has(1), raw, -1), place_of)
    named = place_of.astype(jnp.float32)
    for side in range(2):
        meta[side, 0:16] = named[16 * side : 16 * side + 16]
        for row, table in ((16, capacity), (24, diag)):
            for pair in range(2):
                meta[side, row + 4 * pair : row + 4 * pair + 4] = table[
                    side, 0:4, pair * LANES : (pair + 1) * LANES
                ]
    for side in range(2):

        @pl.when(has(side))
        def _():
            row_facts(side).start()
            matrix_rows(side).start()

    for pair in range(4):
        wanted = [named[8 * pair + k : 8 * pair + k + 1] for k in range(7)]

        def build(place, carry, pair=pair, wanted=wanted):
            name = place.astype(jnp.float32)
            tile = jnp.where(wanted[0] == name, turned[pair, 0], 0.0)
            for k in range(1, 7):
                tile = tile + jnp.where(wanted[k] == name, turned[pair, k], 0.0)
            high, low = split(tile)
            at = pl.ds(pl.multiple_of(place * BLOCK, BLOCK), BLOCK)
            lanes = slice(pair % 2 * LANES, (pair % 2 + 1) * LANES)
            mat_high[pair // 2, at, lanes] = high
            mat_low[pair // 2, at, lanes] = low
            return carry

        lax.fori_loop(0, 16, build, 0)

    def pieces_of(value):
        high, low = split(value)
        return high, jnp.concatenate([high, low], axis=0)

    def times(pieces, matrix_high, matrix_low):
        high, stacked = pieces
        both = jnp.dot(stacked, matrix_high, preferred_element_type=jnp.float32)
        rest = jnp.dot(high, matrix_low, preferred_element_type=jnp.float32)
        return both[:STEPS] + both[STEPS:] + rest

    def rows_of(side):
        return pl.ds(pl.multiple_of(side * (4 * BLOCK), 4 * BLOCK), 4 * BLOCK)

    def received(pieces, half, side):
        rows = rows_of(2 + side)
        return times(pieces, mat_high[half, rows, :], mat_low[half, rows, :])

    def face(value, side, from_side):
        rows = rows_of(from_side)
        return times(pieces_of(value), face_high[side, rows, :], face_low[side, rows, :])

    real_rows = lax.broadcasted_iota(jnp.int32, (STEPS, 1), 0) <= HALF
    last = coefs[:, 2:3]

    def note(value, half):
        total[half] += value
        weighted = value * last
        tails[half] += weighted[0:8] + weighted[8:16] + weighted[16:24] + weighted[24:32]

    def own_product(pieces, half, application):
        closes = lax.rem(application, SWEEPS) == SWEEPS - 1
        tail = jnp.sum(tails[half], axis=0, keepdims=True)
        fix = jnp.where(closes, tail, 0.0) * capacity[half, 0:1]
        tails[half] = jnp.where(closes, 0.0, tails[half])
        result = times(
            pieces, mat_high[half, 0 : 8 * BLOCK, :], mat_low[half, 0 : 8 * BLOCK, :]
        )
        return result - jnp.where(real_rows, fix, 0.0)

    far_waits = (lax.rem(shard, 4) == 1) | (lax.rem(shard, 4) == 2)

    def send_field(slot, side, paired):
        @pl.when(has(side) & jnp.logical_not(far_waits))
        def _():
            field_near(slot, side).start()

        if paired:

            @pl.when(has_far(side))
            def _():
                field_far(slot, side).start()

        @pl.when(has(side) & far_waits)
        def _():
            field_near(slot, side).start()

    def advance(slot, slow_part, fast_part, pieces, application, paired):
        for half, value in ((slow, slow_part), (fast, fast_part)):
            value = divided(value + received(pieces, half, slow), half)
            wsend[slot, half] = value
            if half is slow:
                send_field(slot, half, paired)
            note(value, half)
        pieces = pieces_of(jnp.concatenate([wsend[slot, 0], wsend[slot, 1]], axis=1))
        for half in (slow, fast):
            result = own_product(pieces, half, application)
            own_part[slot, half] = result
            if paired:
                part_send[slot, half] = divided(result, half)

                @pl.when(has(half))
                def _():
                    part_near(slot, half).start()

            if half is slow:
                send_field(slot, fast, paired)

    def near_of(slot, side):
        @pl.when(has(side))
        def _():
            field_near(slot, 1 - side).wait_recv()

        return pieces_of(near[slot, side])

    def add_fast(slow_part, fast_part, pieces):
        return slow_part + received(pieces, slow, fast), fast_part + received(pieces, fast, fast)

    def begun(slot):
        return add_fast(own_part[slot, slow], own_part[slot, fast], near_of(slot, fast))

    total[...] = jnp.zeros_like(total)
    tails[...] = jnp.zeros_like(tails)
    first_own.wait_recv()
    halves = [psend[group, half] + pown[half] for half in range(2)]
    for half in range(2):
        note(halves[half], half)
    pieces = pieces_of(jnp.concatenate(halves, axis=1))
    slow_part = own_product(pieces, slow, jnp.int32(0))
    fast_part = own_product(pieces, fast, jnp.int32(0))
    for side in order:

        @pl.when(has(side))
        def _():
            for sender in range(2):
                first_halo(1 - side, 0, sender).wait_recv()

        pieces = pieces_of(precv[0, side] + precv[1, side])
        if side is fast:
            slow_part, fast_part = add_fast(slow_part, fast_part, pieces)
    advance(0, slow_part, fast_part, pieces, jnp.int32(1), False)

    advance(1, *begun(0), near_of(0, slow), jnp.int32(2), True)

    for side in range(2):

        @pl.when(has(side))
        def _():
            matrix_rows(1 - side).wait_recv()
            passed_on(side).start()

    for side in range(2):

        @pl.when(has(side))
        def _():
            row_facts(1 - side).wait_recv()

        face_recip[side, 0], face_recip[side, 1], face_recip[side, 2] = reciprocals(
            jnp.concatenate([met[side, 16:17], met[side, 20:21]], axis=1),
            jnp.concatenate([met[side, 24:25], met[side, 28:29]], axis=1),
        )

        @pl.when(has(side))
        def _():
            passed_on(side).wait_recv()

        for pair in range(2):

            def build(place, carry, side=side, pair=pair):
                name = (place + 8).astype(jnp.float32)
                tile = jnp.where(
                    met[side, 8 * pair + 1 : 8 * pair + 2] == name, tiles[side, pair, 0], 0.0
                )
                for k in range(2, 7):
                    wanted = met[side, 8 * pair + k : 8 * pair + k + 1]
                    tile = tile + jnp.where(wanted == name, tiles[side, pair, k - 1], 0.0)
                high, low = split(tile)
                at = pl.ds(pl.multiple_of(place * BLOCK, BLOCK), BLOCK)
                face_high[side, at, pair * LANES : (pair + 1) * LANES] = high
                face_low[side, at, pair * LANES : (pair + 1) * LANES] = low
                return carry

            lax.fori_loop(0, 8, build, 0)

    def ahead_of(slot, side, early):
        @pl.when(has_far(side))
        def _():
            field_far(slot, 1 - side).wait_recv()

        found = divide(
            early + face(far[slot, side], side, side),
            face_recip[side, 0], face_recip[side, 1], face_recip[side, 2],
        )

        @pl.when(has(side))
        def _():
            part_near(slot, 1 - side).wait_recv()

        return pieces_of(found + part[slot, side])

    def couple(slot):
        early = [face(wsend[slot, side], side, 1 - side) for side in order]
        slow_part, fast_part = begun(slot)
        pieces = ahead_of(slot, fast, early[0])
        slow_more, fast_more = received(pieces, slow, fast), received(pieces, fast, fast)
        pieces = near_of(slot, slow)
        for half, value in ((slow, slow_part), (fast, fast_part)):
            value = divided(value + received(pieces, half, slow), half)
            middle[half] = value
            note(value, half)
        pieces = pieces_of(jnp.concatenate([middle[0], middle[1]], axis=1))
        slow_part = slow_more + own_product(pieces, slow, 2 * slot + 1)
        fast_part = fast_more + own_product(pieces, fast, 2 * slot + 1)
        return slow_part, fast_part, ahead_of(slot, slow, early[1])

    def step(slot, carry):
        advance(slot + 1, *couple(slot), 2 * slot + 2, True)
        return carry

    lax.fori_loop(1, PAIRS, step, 0)
    slow_part, fast_part, pieces = couple(PAIRS)
    for half, value in ((slow, slow_part), (fast, fast_part)):
        total[half] += divided(value + received(pieces, half, slow), half)

    places = []
    for block in range(8):
        place = jnp.int32(0)
        for i in range(1, 8):
            place = place + jnp.where(ids[i] == block, i, 0)
        places.append(place)
    summed = product(backward[...], reorder(jnp.concatenate([total[0], total[1]], axis=1), places))
    early, late = summed[:HALF], summed[HALF:]
    ysend[...] = jnp.where(first, late, early)
    ycopy = remote(ysend, yrecv, last_sems.at[0], last_sems.at[1], (other, shard))
    ycopy.start()

    first_own.wait_send()
    for side in range(2):

        @pl.when(has(side))
        def _():
            for case in range(2):
                first_halo(side, case, group).wait_send()
            matrix_rows(side).wait_send()
            row_facts(side).wait_send()
            passed_on(side).wait_send()
            for slot in range(PAIRS + 1):
                field_near(slot, side).wait_send()
            for slot in range(1, PAIRS + 1):
                part_near(slot, side).wait_send()

        @pl.when(has_far(side))
        def _():
            for slot in range(1, PAIRS + 1):
                field_far(slot, side).wait_send()

    kept = jnp.where(first, early, late)
    ycopy.wait()
    came = yrecv[...]
    out[:, 0, :] = jnp.where(first, kept, came)
    out[:, 1, :] = jnp.where(first, came, kept)


def per_device(adj_source, terminal, capacity, blocks, columns, face_lists):
    nodes = capacity.shape[0]
    half = nodes // 2
    forward, backward, coefs = tables()
    hbm = pl.BlockSpec(memory_space=pltpu.HBM)
    f32, bf16, i32 = jnp.float32, jnp.bfloat16, jnp.int32
    dma = pltpu.SemaphoreType.DMA
    return pl.pallas_call(
        kernel,
        out_shape=pltpu.VMEM(adj_source.shape, f32),
        in_specs=[hbm] * 9,
        out_specs=pl.BlockSpec(memory_space=pltpu.VMEM),
        scratch_shapes=[
            pltpu.VMEM(adj_source.shape, f32),
            pltpu.VMEM(terminal.shape, f32),
            pltpu.VMEM((1, nodes), f32),
            pltpu.SMEM(columns.shape, i32),
            pltpu.SMEM(face_lists.shape, i32),
            pltpu.VMEM(forward.shape, bf16),
            pltpu.VMEM(backward.shape, bf16),
            pltpu.VMEM(coefs.shape, f32),
            pltpu.VMEM((8, BLOCK, BLOCK), f32),
            pltpu.VMEM((8, 6, BLOCK, BLOCK), f32),
            pltpu.VMEM((4, 7, BLOCK, LANES), f32),
            pltpu.VMEM((32, LANES), i32),
            pltpu.VMEM((2, 16 * BLOCK, half), bf16),
            pltpu.VMEM((2, 16 * BLOCK, half), bf16),
            pltpu.VMEM((2, 8 * BLOCK, half), bf16),
            pltpu.VMEM((2, 8 * BLOCK, half), bf16),
            pltpu.VMEM((2, 8, half), f32),
            pltpu.VMEM((2, 3, HALF, half), f32),
            pltpu.VMEM((2, 3, HALF, half), f32),
            pltpu.VMEM((2, 8, half), f32),
            pltpu.VMEM((2, 32, LANES), f32),
            pltpu.VMEM((2, 32, LANES), f32),
            pltpu.VMEM((2, 2, 6, BLOCK, LANES), f32),
            pltpu.VMEM((2, 2, STEPS, half), f32),
            pltpu.VMEM((2, 2, STEPS, half), f32),
            pltpu.VMEM((2, STEPS, half), f32),
            pltpu.VMEM((PAIRS + 1, 2, STEPS, half), f32),
            pltpu.VMEM((PAIRS + 1, 2, STEPS, half), f32),
            pltpu.VMEM((PAIRS + 1, 2, STEPS, half), f32),
            pltpu.VMEM((PAIRS + 1, 2, STEPS, half), f32),
            pltpu.VMEM((PAIRS + 1, 2, STEPS, half), f32),
            pltpu.VMEM((PAIRS + 1, 2, STEPS, half), f32),
            pltpu.VMEM((2, STEPS, half), f32),
            pltpu.VMEM((2, 8, half), f32),
            pltpu.VMEM((2, STEPS, half), f32),
            pltpu.VMEM((HALF, nodes), f32),
            pltpu.VMEM((HALF, nodes), f32),
            dma((10,)),
            dma((5,)),
            dma((5,)),
            dma((6,)),
            dma((6,)),
            dma((2,)),
            dma((PAIRS + 1, 3, 2)),
            dma((PAIRS + 1, 3, 2)),
        ],
        compiler_params=pltpu.CompilerParams(
            collective_id=0, has_side_effects=True, vmem_limit_bytes=60 * 1024 * 1024
        ),
        name="window",
    )(
        adj_source, terminal, capacity.reshape(1, nodes), columns, face_lists,
        jnp.asarray(forward), jnp.asarray(backward), jnp.asarray(coefs), blocks,
    )


def solution(mesh):
    return jax.shard_map(
        per_device,
        mesh=mesh,
        in_specs=(
            P("tm", None, "space"),
            P(None, "space"),
            P("space"),
            P("space", None, None, None),
            P("space", None),
            P("space", None, None),
        ),
        out_specs=P("tm", None, "space"),
        check_vma=False,
    )
```
